512 devices in a mesh: dp: 16 (over y, x), expert: 32 (over z, core).
Axes of the slice: x: 4, y: 4, z: 16, core: 2. Of those that a mesh axis runs over, the one named last changes fastest.
Arguments:
- tokens: bfloat16 [65536, 2048], P(('dp', 'expert')), may hold values from -6 to 6
- cotangent: bfloat16 [65536, 2048], P(('dp', 'expert')), may hold values from -12 to 12
- routes: int32 [65536, 2], P(('dp', 'expert')), may hold values from 0 to 31, all different within a row; in each aligned block of 128 rows (0 to 127, 128 to 255, ...) at most 10 rows name the same one
- route_weight: float32 [65536, 2], P(('dp', 'expert')), may hold values from 0.2 to 1
- w_gate: bfloat16 [32, 2048, 768], P('expert', 'dp'), may hold values from -0.125 to 0.125
- w_up: bfloat16 [32, 2048, 768], P('expert', 'dp'), may hold values from -0.125 to 0.125
- w_down: bfloat16 [32, 768, 2048], P('expert', None, 'dp'), may hold values from -0.21875 to 0.21875
Outputs:
- mixed: bfloat16 [65536, 2048], P(('dp', 'expert'))
- grad_tokens: bfloat16 [65536, 2048], P(('dp', 'expert'))
- route_grad: float32 [65536, 2], P(('dp', 'expert'))
- grad_down: float32 [32, 768, 2048], P('expert', None, 'dp')
The draws below stay inside these ranges and needn't reach their ends.
Inputs may be any that keep to these rules, and one draw needn't show every extreme that they name: `routes`: each row names 2 different experts. Within the rows of one device (aligned blocks of 128 tokens) no expert is named more than 10 times, a bound that some block reaches.
All inputs are finite; a program needn't handle non-finite values.
Results may differ from the reference program's by a relative error of at most 0.015.
Values may be sent and summed in bfloat16 or wider, within the bound.
A program may use at most 64 MiB of HBM per device.

```python
import math
import jax
import jax.numpy as jnp
import numpy as np
from jax import lax

D = 2048
FF = 768
TOPK = 2
TOK_DEV = 128
EXPERTS = 32
CAP = 10
TOKENS = 65536
N_DP = 16
N_EXPERT = 32


def with_spikes(entries, stream_key, source, target, shards_of, factor):
    owner, partner = [(jnp.arange(entries.shape[dim]) // (entries.shape[dim] // shards_of)).reshape([-1 if axis == dim else 1 for axis in range(entries.ndim)]) for dim in (source, target)]
    chosen = jax.random.permutation(stream_key, shards_of)[partner]
    strong = (owner == chosen) | (owner == (partner + shards_of // 2) % shards_of)
    return jnp.where(strong, factor * entries, entries)


def steps_of(own_key, shape, cuts, smallest, high):
    gain, own = 1.0, jax.random.fold_in(own_key, 6)
    for dim, shards_of in cuts:
        steps = jnp.exp(jax.random.uniform(jax.random.fold_in(own, dim), (shards_of,), jnp.float32, smallest / len(cuts), high / len(cuts)))
        gain = gain * jnp.repeat(steps, shape[dim] // shards_of).reshape([-1 if axis == dim else 1 for axis in range(len(shape))])
    return gain


def deal_out(rng, own, number, rows, count, top, bound, skew):
    order = jax.random.permutation(rng, count)
    heavy_load, ordinary = shares(count, rows * top, bound, skew, True), shares(count, rows * top, bound, skew, False)
    places = jnp.arange(count)

    def named(tallies, offset_by):
        used = int((tallies > 0).sum())
        fixed = max(1, used // 4)
        passed = fixed + (places - fixed + offset_by * (used - fixed)) % max(1, count - fixed)
        return jnp.zeros((count,), jnp.int32).at[order[jnp.where(places < fixed, places, passed)]].set(jnp.asarray(tallies, jnp.int32))

    tallies = jnp.where(number % 4 == 0, named(heavy_load, number // 4), named(ordinary, number - number // 4 - 1))
    mixed = jax.random.permutation(jax.random.fold_in(own, 3), count)
    giver, sink = mixed[0:count // 2 * 2:2], mixed[1:count // 2 * 2:2]
    slack = jnp.minimum(tallies[giver] - 1, bound - tallies[sink]) // 2
    slack = jnp.where((giver == order[0]) | (sink == order[0]) | (tallies[sink] == 0), 0, jnp.maximum(slack, 0))
    passed = jax.random.randint(jax.random.fold_in(own, 4), (count // 2,), 0, 1 << 20) % (slack + 1)
    tallies = tallies.at[giver].add(-passed).at[sink].add(passed)
    items = jnp.searchsorted(jnp.cumsum(tallies), jnp.arange(rows * top), side="right").astype(jnp.int32)
    table = items.reshape(top, rows).T
    table = table[jax.random.permutation(jax.random.fold_in(own, 1), rows)]
    offset_by = jax.random.randint(jax.random.fold_in(own, 2), (rows, 1), 0, top)
    return jnp.take_along_axis(table, (jnp.arange(top)[None, :] + offset_by) % top, axis=1)


def shares(number_of, total, bound, slope, full):
    weights = [(1 << 20) // math.isqrt(rank ** slope) + 1 for rank in range(1, number_of + 1)]
    largest = bound if full else min(bound, max(-(-total // number_of), total * weights[0] // sum(weights)))
    least = 1 if total - largest >= number_of - 1 else 0
    counts, spare = [largest] + [least] * (number_of - 1), total - largest - least * (number_of - 1)
    while spare > 0:
        candidates = [i for i in range(1, number_of) if counts[i] < largest] or [i for i in range(1, number_of) if counts[i] < bound]
        pool, budget = sum([weights[i] for i in candidates]), spare
        for i in candidates:
            addition = min(bound - counts[i], max(1, budget * weights[i] // pool), spare)
            counts[i] = counts[i] + addition
            spare = spare - addition
    return np.array(counts)


def centred(stream_key, dims, width, limit, shards=(), kind=jnp.bfloat16):
    factor_of = steps_of(stream_key, dims, shards, -0.22, 0.18) if shards else 1.0
    values = jax.random.normal(stream_key, dims, jnp.float32) * width * factor_of
    return jnp.minimum(jnp.maximum(values, -limit), limit).astype(kind)


def noise_with(key, extent, spread, reach, split, heavy, kind=jnp.bfloat16):
    values = spread * jax.random.normal(key, extent, jnp.float32)
    if split:
        values = values * steps_of(key, extent, split, -0.22, 0.18)
    return jnp.clip(with_spikes(values, jax.random.fold_in(key, 3), *heavy), -reach, reach).astype(kind)


def setup_inputs(seed: int = 0) -> dict:
    seeds = jax.random.split(jax.random.key(seed), 8)
    tokens = centred(seeds[0], (TOKENS, D), 1.0, 6.0, ((0, 512),))
    cotangent = noise_with(seeds[1], (TOKENS, D), 0.5, 12.0, ((0, 512),), (0, 1, 512, 6.0))
    routes_keys = jax.random.split(jax.random.fold_in(seeds[2], 1), TOKENS // TOK_DEV)
    routes_turns = jax.random.permutation(jax.random.fold_in(seeds[2], 3), TOKENS // TOK_DEV)
    routes = jax.vmap(lambda own, number: deal_out(jax.random.fold_in(seeds[2], 2), own, number, TOK_DEV, EXPERTS, TOPK, CAP, 2))(routes_keys, routes_turns).reshape((TOKENS, TOPK))
    route_weight = jnp.clip(jnp.exp(math.log(1.0) - 1.609438 * jax.random.uniform(seeds[3], (TOKENS, TOPK), jnp.float32) ** steps_of(seeds[3], (TOKENS, TOPK), ((0, 512),), -0.2, 0.2)), 0.2, 1.0)
    w_gate = centred(seeds[4], (EXPERTS, D, FF), D ** -0.5, 0.125, ((0, 32), (1, 16)))
    w_up = centred(seeds[5], (EXPERTS, D, FF), D ** -0.5, 0.125, ((0, 32), (1, 16)))
    w_down = centred(seeds[6], (EXPERTS, FF, D), FF ** -0.5, 0.21875, ((0, 32), (2, 16)))
    return dict(tokens=tokens, cotangent=cotangent, routes=routes, route_weight=route_weight, w_gate=w_gate, w_up=w_up, w_down=w_down)


def slot_table(routes):
    blocks = TOKENS // TOK_DEV
    pair_count = TOK_DEV * TOPK
    flat_routes = routes.reshape(blocks, pair_count).astype(jnp.int32)
    one_hot = (flat_routes[:, :, None] == jnp.arange(EXPERTS, dtype=jnp.int32)[None, None, :]).astype(jnp.int32)
    earlier = (jnp.cumsum(one_hot, axis=1) - one_hot).astype(jnp.int32)
    slot_index = jnp.sum(earlier * one_hot, axis=2).astype(jnp.int32)
    block_id = jnp.broadcast_to(jnp.arange(blocks, dtype=jnp.int32)[:, None], (blocks, pair_count))
    group_id = (block_id // N_EXPERT).astype(jnp.int32)
    position = ((block_id % N_EXPERT) * CAP + slot_index).astype(jnp.int32)
    pair_id = (block_id * pair_count + jnp.arange(pair_count, dtype=jnp.int32)[None, :]).astype(jnp.int32)
    table = jnp.full((EXPERTS, N_DP, N_EXPERT * CAP), TOKENS * TOPK, jnp.int32)
    return table.at[flat_routes, group_id, position].set(pair_id)


def reference(tokens, cotangent, routes, route_weight, w_gate, w_up, w_down):
    total_pairs = TOKENS * TOPK
    table = slot_table(routes)
    tokens_ext = jnp.concatenate([tokens, jnp.zeros((1, D), tokens.dtype)], axis=0)
    cot_ext = jnp.concatenate([cotangent, jnp.zeros((1, D), cotangent.dtype)], axis=0)
    weight_ext = jnp.concatenate([route_weight.reshape(-1), jnp.zeros((1,), route_weight.dtype)], axis=0)
    row_count = N_DP * N_EXPERT * CAP

    def expert_step(state, expert_id):
        out_acc, back_acc = state
        pair_ids = table[expert_id].reshape(row_count)
        token_ids = (pair_ids // TOPK).astype(jnp.int32)
        inputs = tokens_ext[token_ids]
        scaled = (weight_ext[pair_ids][:, None] * cot_ext[token_ids].astype(jnp.float32)).astype(jnp.bfloat16)
        gate_w = w_gate[expert_id]
        up_w = w_up[expert_id]
        down_w = w_down[expert_id]
        gate_pre = jnp.dot(inputs, gate_w, preferred_element_type=jnp.float32)
        up_pre = jnp.dot(inputs, up_w, preferred_element_type=jnp.float32)
        sigma = jax.nn.sigmoid(gate_pre)
        activated = gate_pre * sigma
        hidden = (activated * up_pre).astype(jnp.bfloat16)
        outputs = jnp.dot(hidden, down_w, preferred_element_type=jnp.float32).astype(jnp.bfloat16)
        grad_hidden = jnp.dot(scaled, down_w.T, preferred_element_type=jnp.float32)
        grad_gate = (grad_hidden * up_pre * sigma * (1.0 + gate_pre * (1.0 - sigma))).astype(jnp.bfloat16)
        grad_up = (grad_hidden * activated).astype(jnp.bfloat16)
        grad_rows = (jnp.dot(grad_gate, gate_w.T, preferred_element_type=jnp.float32)
                     + jnp.dot(grad_up, up_w.T, preferred_element_type=jnp.float32)).astype(jnp.bfloat16)
        partial_sums = jnp.einsum("grf,grd->gfd",
                                  hidden.reshape(N_DP, N_EXPERT * CAP, FF).astype(jnp.float32),
                                  scaled.reshape(N_DP, N_EXPERT * CAP, D).astype(jnp.float32))
        rounded = lax.optimization_barrier(partial_sums.astype(jnp.bfloat16))
        grad_expert = jnp.sum(rounded.astype(jnp.float32), axis=0)
        out_acc = out_acc.at[pair_ids].set(outputs)
        back_acc = back_acc.at[pair_ids].set(grad_rows)
        return (out_acc, back_acc), grad_expert

    start_state = (jnp.zeros((total_pairs + 1, D), jnp.bfloat16), jnp.zeros((total_pairs + 1, D), jnp.bfloat16))
    final_state, grad_down = lax.scan(expert_step, start_state, jnp.arange(EXPERTS, dtype=jnp.int32))
    out_pairs = final_state[0][:total_pairs].reshape(TOKENS, TOPK, D).astype(jnp.float32)
    back_pairs = final_state[1][:total_pairs].reshape(TOKENS, TOPK, D).astype(jnp.float32)
    mixed = jnp.sum(route_weight[:, :, None] * out_pairs, axis=1).astype(jnp.bfloat16)
    route_grad = jnp.sum(cotangent.astype(jnp.float32)[:, None, :] * out_pairs, axis=2)
    grad_tokens = jnp.sum(back_pairs, axis=1).astype(jnp.bfloat16)
    return (mixed, grad_tokens, route_grad, grad_down)
```

```python
import functools
import jax
import jax.numpy as jnp
from jax import lax
from jax.experimental import pallas as pl
from jax.experimental.pallas import tpu as pltpu
from jax.sharding import PartitionSpec as P

CAP = 10
BF = jnp.bfloat16
F32 = jnp.float32
PLANE = [(1, 0), (0, 1), (3, 0), (0, 3), (2, 0), (0, 2), (1, 1), (3, 3),
         (1, 3), (3, 1), (2, 1), (1, 2), (2, 3), (3, 2), (2, 2)]


def dot_nn(a, b):
    return lax.dot_general(a, b, (((1,), (0,)), ((), ())), preferred_element_type=F32)


def dot_nt(a, b):
    return lax.dot_general(a, b, (((1,), (1,)), ((), ())), preferred_element_type=F32)


def iota(shape, dim):
    return lax.broadcasted_iota(jnp.int32, shape, dim)


def kernel(routes, rw, x, cot, wg, wu, wd, mixed, gtok, rgrad, gdown,
           W, sx, sc, rx, rc, RX, RC, H, GG, GU, OO, GP, po, pg, ro, rg, UO, UG, GT, GR, S,
           wss, wrs, tss, trs, bss, brs, gss, grs):
    g = lax.axis_index("dp")
    s = lax.axis_index("expert")
    z, c = s // 2, lax.rem(s, 2)
    px, py = lax.rem(g, 4), g // 4
    me_e = s

    def plane(d):
        return lax.rem(py + d[1], 4) * 4 + lax.rem(px + d[0], 4)

    def dz(pos):
        return jnp.where(lax.rem(pos, 2) == 1, (pos + 1) // 2, 16 - pos // 2)

    bar = pltpu.get_barrier_semaphore()

    @pl.loop(1, 32)
    def _(d):
        pl.semaphore_signal(bar, inc=1, device_id=(g, lax.rem(s + d, 32)))

    for d in PLANE:
        pl.semaphore_signal(bar, inc=1, device_id=(plane(d), s))

    eye = (iota((128, 128), 0) == iota((128, 128), 1))
    eyeb = eye.astype(BF)
    W[g, 0:128] = wg[...]
    W[g, 128:256] = wu[...]
    W[g, 256:384] = dot_nt(eyeb, wd[...]).astype(BF)

    pl.semaphore_wait(bar, 31 + 15)

    def w_copy(i, r, n):
        return pltpu.make_async_remote_copy(
            W.at[g, pl.ds(r, n)], W.at[g, pl.ds(r, n)], wss.at[i], wrs.at[i],
            device_id=(plane(PLANE[i]), s))

    @pl.loop(0, 12)
    def _(p):
        for i in range(15):
            w_copy(i, p * 32, 32).start()

    lanes = iota((128, 128), 1)
    r0, r1 = routes[:, 0:1], routes[:, 1:2]
    h0, h1 = (lanes == r0), (lanes == r1)
    named = (h0.astype(F32) + h1.astype(F32)).astype(BF)
    before = (iota((128, 128), 0) > lanes).astype(BF)
    count = dot_nn(before, named)
    t0 = r0.astype(F32) * CAP + jnp.sum(jnp.where(h0, count, 0.0), axis=1, keepdims=True)
    t1 = r1.astype(F32) * CAP + jnp.sum(jnp.where(h1, count, 0.0), axis=1, keepdims=True)
    u0 = jnp.sum(jnp.where(eye, t0, 0.0), axis=0, keepdims=True)
    u1 = jnp.sum(jnp.where(eye, t1, 0.0), axis=0, keepdims=True)
    slots = iota((384, 128), 0).astype(F32)
    P0, P1 = (slots == u0).astype(BF), (slots == u1).astype(BF)

    S[...] = (iota((256, 256), 1) == lax.rem(iota((256, 256), 0), 16) * 16
              + iota((256, 256), 0) // 16).astype(BF)

    def pack(src, dst, lo, n):
        @pl.loop(0, n)
        def _(q):
            r = pl.multiple_of(lo + q * 32, 32)
            a = src[pl.ds(r, 32), :]
            cols = [jnp.concatenate([a[h * 16:h * 16 + 16, k * 128:k * 128 + 128] for k in range(16)], axis=0)
                    for h in range(2)]
            o = dot_nn(S[...], jnp.concatenate(cols, axis=1)).astype(BF)
            dst[pl.ds(r, 16)] = o[:, :128].reshape(16, 16, 128)
            dst[pl.ds(r + 16, 16)] = o[:, 128:].reshape(16, 16, 128)

    def unpack(src, dst, lo, n):
        @pl.loop(0, n)
        def _(q):
            r = pl.multiple_of(lo + q * 32, 32)
            a = src[pl.ds(r, 32)].reshape(512, 128)
            o = dot_nn(S[...], jnp.concatenate([a[:256], a[256:]], axis=1)).astype(BF)
            for h in range(2):
                dst[pl.ds(r + h * 16, 16), :] = jnp.concatenate(
                    [o[k * 16:k * 16 + 16, h * 128:h * 128 + 128] for k in range(16)], axis=1)

    def tok(kind, pos, hc):
        src, dst = ((sx, rx), (sc, rc))[kind]
        e = lax.rem(z + dz(pos), 16) * 2 + hc
        return pltpu.make_async_remote_copy(
            src.at[pl.ds(e * CAP, CAP)], dst.at[pl.ds((2 * pos + c) * CAP, CAP)],
            tss.at[kind, 2 * pos + hc], trs.at[kind, 2 * pos + c], device_id=(g, e))

    def tok_recv(kind, q):
        src, dst = ((sx, rx), (sc, rc))[kind]
        return pltpu.make_async_remote_copy(
            src.at[pl.ds(0, CAP)], dst.at[pl.ds(q * CAP, CAP)],
            tss.at[kind, q], trs.at[kind, q], device_id=(g, s + 1 - 2 * c))

    def send_tokens(kind):
        src, dst = ((sx, rx), (sc, rc))[kind]
        tok(kind, 0, 1 - c).start()

        @pl.loop(1, 16)
        def _(pos):
            tok(kind, pos, 0).start()
            tok(kind, pos, 1).start()
        dst[pl.ds(c * CAP, CAP)] = src[pl.ds(me_e * CAP, CAP)]

    pa = (P0.astype(F32) + P1.astype(F32)).astype(BF)

    @pl.loop(0, 8)
    def _(m):
        k = pl.ds(pl.multiple_of(m * 256, 256), 256)
        UO[:, k] = dot_nn(pa, x[:, k]).astype(BF)
    pack(UO, sx, 0, 10)
    send_tokens(0)

    @pl.loop(0, 8)
    def _(m):
        k = pl.ds(pl.multiple_of(m * 256, 256), 256)
        cf = cot[:, k].astype(F32)
        v0 = (cf * rw[:, 0:1]).astype(BF)
        v1 = (cf * rw[:, 1:2]).astype(BF)
        UG[:, k] = (dot_nn(P0, v0) + dot_nn(P1, v1)).astype(BF)
    pack(UG, sc, 0, 10)
    send_tokens(1)

    for i in range(15):
        w_copy(i, 0, 384).wait_recv()

    def back(kind, pos, cc):
        src, dst = ((po, ro), (pg, rg))[kind]
        t = lax.rem(z + 16 - lax.rem(dz(pos), 16), 16) * 2 + cc
        return pltpu.make_async_remote_copy(
            src.at[pl.ds((2 * pos + cc) * CAP, CAP)], dst.at[pl.ds(me_e * CAP, CAP)],
            bss.at[kind, 2 * pos + cc], brs.at[kind, me_e], device_id=(g, t))

    def back_recv(kind, e):
        src, dst = ((po, ro), (pg, rg))[kind]
        return pltpu.make_async_remote_copy(
            src.at[pl.ds(0, CAP)], dst.at[pl.ds(e * CAP, CAP)],
            bss.at[kind, e], brs.at[kind, e], device_id=(g, s + 1 - 2 * c))

    for half in range(2):
        for kind in range(2):
            if half == 0:
                tok_recv(kind, 1 - c).wait_recv()

            @pl.loop(half * 16 + (2 if half == 0 else 0), half * 16 + 16)
            def _(q):
                tok_recv(kind, q).wait_recv()
        lo = half * 160
        unpack(rx, RX, lo, 5)
        unpack(rc, RC, lo, 5)
        rows = pl.ds(lo, 160)

        @pl.loop(0, 3)
        def _(n):
            k = pl.ds(pl.multiple_of(n * 256, 256), 256)
            xs, cs = RX[rows, :], RC[rows, :]
            gate = dot_nn(xs, W[:, 0:128, k].reshape(2048, 256))
            up = dot_nn(xs, W[:, 128:256, k].reshape(2048, 256))
            gh = dot_nn(cs, W[:, 256:384, k].reshape(2048, 256))
            sig = jax.nn.sigmoid(gate)
            act = gate * sig
            H[rows, k] = (act * up).astype(BF)
            GG[rows, k] = (gh * up * sig * (1.0 + gate * (1.0 - sig))).astype(BF)
            GU[rows, k] = (gh * act).astype(BF)

        @pl.loop(0, 8)
        def _(m):
            k = pl.ds(pl.multiple_of(m * 256, 256), 256)
            j = pl.ds(2 * m, 2)
            OO[rows, k] = dot_nt(H[rows, :], W[j, 256:384, :].reshape(256, 768)).astype(BF)
            GP[rows, k] = (dot_nt(GG[rows, :], W[j, 0:128, :].reshape(256, 768))
                           + dot_nt(GU[rows, :], W[j, 128:256, :].reshape(256, 768))).astype(BF)
        for kind in range(2):
            src, dst, flat = ((po, ro, OO), (pg, rg, GP))[kind]
            pack(flat, src, lo, 5)
            if half == 0:
                back(kind, 0, 1 - c).start()
                dst[pl.ds(me_e * CAP, CAP)] = src[pl.ds(c * CAP, CAP)]

            @pl.loop(half * 8 + (1 if half == 0 else 0), half * 8 + 8)
            def _(pos):
                back(kind, pos, 0).start()
                back(kind, pos, 1).start()

    HT = jnp.transpose(H[...])

    @pl.loop(0, 8)
    def _(m):
        k = pl.ds(pl.multiple_of(m * 256, 256), 256)
        t = dot_nn(HT, RC[:, k]).astype(BF)
        GT[2 * m] = t[:, :128]
        GT[2 * m + 1] = t[:, 128:]

    def g_copy(i, r, n):
        p = plane(PLANE[i])
        return pltpu.make_async_remote_copy(
            GT.at[p, pl.ds(r, n)], GR.at[i, pl.ds(r, n)], gss.at[i], grs.at[i], device_id=(p, s))

    @pl.loop(0, 4)
    def _(p):
        for i in range(15):
            g_copy(i, p * 192, 192).start()

    slots = iota((128, 384), 1).astype(F32)
    Q0, Q1 = (slots == t0).astype(BF), (slots == t1).astype(BF)
    qa = (Q0.astype(F32) + Q1.astype(F32)).astype(BF)
    UO[320:384, :] = jnp.zeros((64, 2048), BF)
    UG[320:384, :] = jnp.zeros((64, 2048), BF)
    for kind in range(2):
        @pl.loop(0, 32)
        def _(e):
            @pl.when(e != me_e)
            def _():
                back_recv(kind, e).wait_recv()
        if kind == 0:
            unpack(ro, UO, 0, 10)

            def body(m, carry):
                a0, a1 = carry
                k = pl.ds(pl.multiple_of(m * 256, 256), 256)
                o0, o1 = dot_nn(Q0, UO[:, k]), dot_nn(Q1, UO[:, k])
                mixed[:, k] = (rw[:, 0:1] * o0 + rw[:, 1:2] * o1).astype(BF)
                cf = cot[:, k].astype(F32)
                return (a0 + jnp.sum(cf * o0, axis=1, keepdims=True),
                        a1 + jnp.sum(cf * o1, axis=1, keepdims=True))
            a0, a1 = lax.fori_loop(0, 8, body, (jnp.zeros((128, 1), F32), jnp.zeros((128, 1), F32)))
            rgrad[:, 0:1] = a0
            rgrad[:, 1:2] = a1
        else:
            unpack(rg, UG, 0, 10)

            @pl.loop(0, 8)
            def _(m):
                k = pl.ds(pl.multiple_of(m * 256, 256), 256)
                gtok[:, k] = dot_nn(qa, UG[:, k]).astype(BF)

    for i in range(15):
        g_copy(i, 0, 768).wait_recv()

    @pl.loop(0, 12)
    def _(b):
        r = pl.ds(pl.multiple_of(b * 64, 64), 64)
        acc = GT[g, r, :].astype(F32)
        for i in range(15):
            acc = acc + GR[i, r, :].astype(F32)
        gdown[r, :] = acc

    for i in range(15):
        w_copy(i, 0, 384).wait_send()
        g_copy(i, 0, 768).wait_send()
    for kind in range(2):
        tok(kind, 0, 1 - c).wait_send()
        back(kind, 0, 1 - c).wait_send()

        @pl.loop(1, 16)
        def _(pos):
            for h in range(2):
                tok(kind, pos, h).wait_send()
                back(kind, pos, h).wait_send()


def shards(tokens, cotangent, routes, route_weight, w_gate, w_up, w_down):
    rows, width = tokens.shape
    ff = w_gate.shape[2]
    part = w_gate.shape[1]
    tile = lambda: pltpu.VMEM((320, 16, 128), BF)
    flat = lambda n, w: pltpu.VMEM((n, w), BF)
    dma = pltpu.SemaphoreType.DMA
    out = pl.pallas_call(
        kernel,
        out_shape=(
            jax.ShapeDtypeStruct((rows, width), BF),
            jax.ShapeDtypeStruct((rows, width), BF),
            jax.ShapeDtypeStruct((rows, 2), F32),
            jax.ShapeDtypeStruct((ff, part), F32),
        ),
        in_specs=[pl.BlockSpec(memory_space=pltpu.VMEM)] * 7,
        out_specs=[pl.BlockSpec(memory_space=pltpu.VMEM)] * 4,
        scratch_shapes=[
            pltpu.VMEM((16, 384, 768), BF),
            tile(), tile(), tile(), tile(),
            flat(320, 2048), flat(320, 2048),
            flat(320, 768), flat(320, 768), flat(320, 768),
            flat(320, 2048), flat(320, 2048),
            tile(), tile(), tile(), tile(),
            flat(384, 2048), flat(384, 2048),
            pltpu.VMEM((16, 768, 128), BF), pltpu.VMEM((15, 768, 128), BF),
            flat(256, 256),
            dma((15,)), dma((15,)), dma((2, 32)), dma((2, 32)),
            dma((2, 32)), dma((2, 32)), dma((15,)), dma((15,)),
        ],
        compiler_params=pltpu.CompilerParams(
            collective_id=0, has_side_effects=True, vmem_limit_bytes=60 * 2**20),
    )(routes, route_weight, tokens, cotangent, w_gate[0], w_up[0], w_down[0])
    mixed, gtok, rgrad, gdown = out
    return (mixed, gtok, rgrad, gdown[None])


def solution(mesh):
    in_specs = (
        P(("dp", "expert"), None),
        P(("dp", "expert"), None),
        P(("dp", "expert"), None),
        P(("dp", "expert"), None),
        P("expert", "dp", None),
        P("expert", "dp", None),
        P("expert", None, "dp"),
    )
    out_specs = (
        P(("dp", "expert"), None),
        P(("dp", "expert"), None),
        P(("dp", "expert"), None),
        P("expert", None, "dp"),
    )
    return jax.shard_map(shards, mesh=mesh, in_specs=in_specs, out_specs=out_specs, check_vma=False)
```

```python
import functools
import jax
import jax.numpy as jnp
from jax import lax
from jax.experimental import pallas as pl
from jax.experimental.pallas import tpu as pltpu
from jax.sharding import PartitionSpec as P

CAP = 10
BF = jnp.bfloat16
F32 = jnp.float32
PLANE = [(1, 0), (0, 1), (3, 0), (0, 3), (2, 0), (0, 2), (1, 1), (3, 3),
         (1, 3), (3, 1), (2, 1), (1, 2), (2, 3), (3, 2), (2, 2)]


def dot_nn(a, b):
    return lax.dot_general(a, b, (((1,), (0,)), ((), ())), preferred_element_type=F32)


def dot_nt(a, b):
    return lax.dot_general(a, b, (((1,), (1,)), ((), ())), preferred_element_type=F32)


def iota(shape, dim):
    return lax.broadcasted_iota(jnp.int32, shape, dim)


def kernel(routes, rw, x, cot, wg, wu, wd, mixed, gtok, rgrad, gdown,
           W, WZ, sx, sc, rx, rc, RX, RC, H, GG, GU, OO, GP, po, pg, ro, rg, UO, UG, GT, GR, RS, S,
           wss, wrs, zss, zrs, tss, trs, bss, brs, gss, grs, rss, rrs):
    g = lax.axis_index("dp")
    s = lax.axis_index("expert")
    z, c = s // 2, lax.rem(s, 2)
    px, py = lax.rem(g, 4), g // 4
    me_e = jnp.where(c == 0, 2 * z, 2 * g + 1)

    def on_core(n):
        return pl.when(c == n)

    def plane(d):
        return lax.rem(py + d[1], 4) * 4 + lax.rem(px + d[0], 4)

    def dz(pos):
        return jnp.where(lax.rem(pos, 2) == 1, (pos + 1) // 2, lax.rem(16 - pos // 2, 16))

    def up_z(t):
        return lax.rem(z + t + 16, 16)

    bar = pltpu.get_barrier_semaphore()

    @pl.loop(1, 32)
    def _(d):
        pl.semaphore_signal(bar, inc=1, device_id=(g, lax.rem(s + d, 32)))

    @pl.loop(1, 16)
    def _(d):
        pl.semaphore_signal(bar, inc=1, device_id=(lax.rem(g + d, 16), 2 * z))
        pl.semaphore_signal(bar, inc=1, device_id=(lax.rem(g + d, 16), 2 * z + 1))

    eye = (iota((128, 128), 0) == iota((128, 128), 1))
    down_rows = dot_nt(eye.astype(BF), wd[...]).astype(BF)

    @on_core(0)
    def _():
        W[g, 0:128] = wg[...]
        W[g, 128:256] = wu[...]
        W[g, 256:384] = down_rows

    @on_core(1)
    def _():
        WZ[z, 0:128] = wg[...]
        WZ[z, 128:256] = wu[...]
        WZ[z, 256:384] = down_rows

    pl.semaphore_wait(bar, 31 + 30)

    def w_copy(core, i, r, n):
        p = plane(PLANE[i])
        src = W.at[g, pl.ds(r, n)] if core == 0 else WZ.at[p, pl.ds(r, n)]
        return pltpu.make_async_remote_copy(
            src, W.at[g, pl.ds(r, n)], wss.at[i], wrs.at[i], device_id=(p, s))

    def ring(way, t, h):
        to = up_z(1 - 2 * way)
        sl = lax.rem(z + 16 + (t if way else -t), 16)
        r = pl.ds(h * 192, 192)
        return pltpu.make_async_remote_copy(
            WZ.at[sl, r], WZ.at[sl, r], zss.at[way, t, h], zrs.at[way, t, h],
            device_id=(g, 2 * to + 1))

    def relay(t, last):
        for h in range(2):
            for way in range(2):
                ring(way, t - 1, h).wait_recv()
                if not last or h == way:
                    ring(way, t, h).start()

    @on_core(0)
    def _():
        @pl.loop(0, 12)
        def _(p):
            for i in range(15):
                w_copy(0, i, p * 32, 32).start()

    @on_core(1)
    def _():
        for h in range(2):
            for way in range(2):
                ring(way, 0, h).start()

    lanes = iota((128, 128), 1)
    r0, r1 = routes[:, 0:1], routes[:, 1:2]
    h0, h1 = (lanes == r0), (lanes == r1)
    named = (h0.astype(F32) + h1.astype(F32)).astype(BF)
    before = (iota((128, 128), 0) > lanes).astype(BF)
    count = dot_nn(before, named)
    t0 = r0.astype(F32) * CAP + jnp.sum(jnp.where(h0, count, 0.0), axis=1, keepdims=True)
    t1 = r1.astype(F32) * CAP + jnp.sum(jnp.where(h1, count, 0.0), axis=1, keepdims=True)
    u0 = jnp.sum(jnp.where(eye, t0, 0.0), axis=0, keepdims=True)
    u1 = jnp.sum(jnp.where(eye, t1, 0.0), axis=0, keepdims=True)
    slots = iota((384, 128), 0).astype(F32)
    P0, P1 = (slots == u0).astype(BF), (slots == u1).astype(BF)

    S[...] = (iota((256, 256), 1) == lax.rem(iota((256, 256), 0), 16) * 16
              + iota((256, 256), 0) // 16).astype(BF)

    def pack(src, dst, lo, n):
        @pl.loop(0, n)
        def _(q):
            r = pl.multiple_of(lo + q * 32, 32)
            a = src[pl.ds(r, 32), :]
            cols = [jnp.concatenate([a[h * 16:h * 16 + 16, k * 128:k * 128 + 128] for k in range(16)], axis=0)
                    for h in range(2)]
            o = dot_nn(S[...], jnp.concatenate(cols, axis=1)).astype(BF)
            dst[pl.ds(r, 16)] = o[:, :128].reshape(16, 16, 128)
            dst[pl.ds(r + 16, 16)] = o[:, 128:].reshape(16, 16, 128)

    def unpack(src, dst, lo, n):
        @pl.loop(0, n)
        def _(q):
            r = pl.multiple_of(lo + q * 32, 32)
            a = src[pl.ds(r, 32)].reshape(512, 128)
            o = dot_nn(S[...], jnp.concatenate([a[:256], a[256:]], axis=1)).astype(BF)
            for h in range(2):
                dst[pl.ds(r + h * 16, 16), :] = jnp.concatenate(
                    [o[k * 16:k * 16 + 16, h * 128:h * 128 + 128] for k in range(16)], axis=1)

    def chip(pos, sign):
        dx, dy = lax.rem(pos, 4), pos // 4
        return lax.rem(py + sign * dy + 4, 4) * 4 + lax.rem(px + sign * dx + 4, 4)

    def tok(kind, pos, hc):
        src, dst = ((sx, rx), (sc, rc))[kind]
        if hc == 0:
            e = lax.rem(z + dz(pos), 16) * 2
            dev = (g, e)
        else:
            j = chip(pos, 1)
            e = 2 * j + 1
            dev = (j, 2 * z + 1)
        return pltpu.make_async_remote_copy(
            src.at[pl.ds(e * CAP, CAP)], dst.at[pl.ds((2 * pos + c) * CAP, CAP)],
            tss.at[kind, 2 * pos + hc], trs.at[kind, 2 * pos + c], device_id=dev)

    def tok_recv(kind, q):
        src, dst = ((sx, rx), (sc, rc))[kind]
        return pltpu.make_async_remote_copy(
            src.at[pl.ds(0, CAP)], dst.at[pl.ds(q * CAP, CAP)],
            tss.at[kind, q], trs.at[kind, q], device_id=(g, s + 1 - 2 * c))

    def send_tokens(kind, hc, first=0):
        if first == 0:
            @on_core(1 - hc)
            def _():
                tok(kind, 0, hc).start()

        @pl.loop(max(first, 1), 16)
        def _(pos):
            tok(kind, pos, hc).start()

    def keep(kind):
        src, dst = ((sx, rx), (sc, rc))[kind]
        dst[pl.ds(c * CAP, CAP)] = src[pl.ds(me_e * CAP, CAP)]

    pa = (P0.astype(F32) + P1.astype(F32)).astype(BF)

    @pl.loop(0, 8)
    def _(m):
        k = pl.ds(pl.multiple_of(m * 256, 256), 256)
        UO[:, k] = dot_nn(pa, x[:, k]).astype(BF)
    pack(UO, sx, 0, 10)
    keep(0)
    send_tokens(0, 1)

    @on_core(0)
    def _():
        send_tokens(0, 0)

    @on_core(1)
    def _():
        relay(1, False)

    @pl.loop(0, 8)
    def _(m):
        k = pl.ds(pl.multiple_of(m * 256, 256), 256)
        cf = cot[:, k].astype(F32)
        v0 = (cf * rw[:, 0:1]).astype(BF)
        v1 = (cf * rw[:, 1:2]).astype(BF)
        UG[:, k] = (dot_nn(P0, v0) + dot_nn(P1, v1)).astype(BF)
    pack(UG, sc, 0, 10)
    keep(1)
    send_tokens(1, 1)

    @on_core(0)
    def _():
        send_tokens(1, 0)

    @on_core(1)
    def _():
        @pl.loop(2, 7)
        def _(t):
            relay(t, False)
        relay(7, True)
        for way in range(2):
            ring(way, 7, way).wait_recv()
        W[g] = WZ[g]
        for kind in range(2):
            tok(kind, 0, 0).start()

        @pl.loop(0, 12)
        def _(p):
            for i in range(15):
                w_copy(1, i, p * 32, 32).start()
            for kind in range(2):
                tok(kind, p + 1, 0).start()
        for kind in range(2):
            send_tokens(kind, 0, 13)

    for i in range(15):
        w_copy(0, i, 0, 384).wait_recv()

    def back(kind, pos, cc):
        src, dst = ((po, ro), (pg, rg))[kind]
        dev = (jnp.where(c == 0, g, chip(pos, -1)),
               jnp.where(c == 0, lax.rem(z + 16 - dz(pos), 16), z) * 2 + cc)
        return pltpu.make_async_remote_copy(
            src.at[pl.ds((2 * pos + cc) * CAP, CAP)], dst.at[pl.ds(me_e * CAP, CAP)],
            bss.at[kind, 2 * pos + cc], brs.at[kind, me_e], device_id=dev)

    def back_recv(kind, e):
        src, dst = ((po, ro), (pg, rg))[kind]
        return pltpu.make_async_remote_copy(
            src.at[pl.ds(0, CAP)], dst.at[pl.ds(e * CAP, CAP)],
            bss.at[kind, e], brs.at[kind, e], device_id=(g, s + 1 - 2 * c))

    def phase_a(half):
        for kind in range(2):
            if half == 0:
                tok_recv(kind, 1 - c).wait_recv()

            @pl.loop(half * 16 + (2 if half == 0 else 0), half * 16 + 16)
            def _(q):
                tok_recv(kind, q).wait_recv()
        lo = half * 160
        unpack(rx, RX, lo, 5)
        unpack(rc, RC, lo, 5)
        rows = pl.ds(lo, 160)

        @pl.loop(0, 3)
        def _(n):
            k = pl.ds(pl.multiple_of(n * 256, 256), 256)
            xs, cs = RX[rows, :], RC[rows, :]
            gate = dot_nn(xs, W[:, 0:128, k].reshape(2048, 256))
            up = dot_nn(xs, W[:, 128:256, k].reshape(2048, 256))
            gh = dot_nn(cs, W[:, 256:384, k].reshape(2048, 256))
            sig = jax.nn.sigmoid(gate)
            act = gate * sig
            H[rows, k] = (act * up).astype(BF)
            GG[rows, k] = (gh * up * sig * (1.0 + gate * (1.0 - sig))).astype(BF)
            GU[rows, k] = (gh * act).astype(BF)

    def phase_b(half):
        lo = half * 160
        rows = pl.ds(lo, 160)

        @pl.loop(0, 8)
        def _(m):
            k = pl.ds(pl.multiple_of(m * 256, 256), 256)
            j = pl.ds(2 * m, 2)
            OO[rows, k] = dot_nt(H[rows, :], W[j, 256:384, :].reshape(256, 768)).astype(BF)
            GP[rows, k] = (dot_nt(GG[rows, :], W[j, 0:128, :].reshape(256, 768))
                           + dot_nt(GU[rows, :], W[j, 128:256, :].reshape(256, 768))).astype(BF)
        for kind in range(2):
            src, dst, flat = ((po, ro, OO), (pg, rg, GP))[kind]
            pack(flat, src, lo, 5)
            if half == 0:
                back(kind, 0, 1 - c).start()
                dst[pl.ds(me_e * CAP, CAP)] = src[pl.ds(c * CAP, CAP)]

            @pl.loop(half * 8 + (1 if half == 0 else 0), half * 8 + 8)
            def _(pos):
                back(kind, pos, 0).start()
                back(kind, pos, 1).start()

    def g_copy(i, r, n):
        p = plane(PLANE[i])
        return pltpu.make_async_remote_copy(
            GT.at[p, pl.ds(r, n)], GR.at[g, pl.ds(r, n)], gss.at[i], grs.at[g], device_id=(p, s))

    def g_recv(j):
        return pltpu.make_async_remote_copy(
            GT.at[j], GR.at[j], gss.at[0], grs.at[j], device_id=(g, s + 1 - 2 * c))

    def gradients():
        HT = jnp.transpose(H[...])

        @pl.loop(0, 8)
        def _(m):
            k = pl.ds(pl.multiple_of(m * 256, 256), 256)
            t = dot_nn(HT, RC[:, k]).astype(BF)
            GT[2 * m] = t[:, :128]
            GT[2 * m + 1] = t[:, 128:]

        @pl.loop(0, 4)
        def _(p):
            for i in range(15):
                g_copy(i, p * 192, 192).start()
        GR[g] = GT[g]

    def hop(way, t, h, first=False):
        to = up_z(1 - 2 * way)
        j = lax.rem(z + 16 + (t - 7 if way else 8 - t), 16)
        r = pl.ds(h * 384, 384)
        src = GR.at[j, r] if first else RS.at[way, t - 1, r]
        return j, pltpu.make_async_remote_copy(
            src, RS.at[way, t, r], rss.at[way, t, h], rrs.at[way, t, h], device_id=(g, 2 * to + 1))

    def g_wait(j):
        @pl.when(j != g)
        def _():
            g_recv(j).wait_recv()

    def reduce_z():
        for way in range(2):
            for h in range(2):
                j, cp = hop(way, 0, h, True)
                if h == 0:
                    g_wait(j)
                cp.start()

        def step(t, ways):
            for h in range(2):
                for way in ways:
                    j, cp = hop(way, t, h)
                    if h == 0:
                        g_wait(j)
                    hop(way, t - 1, h, True)[1].wait_recv()

                    @pl.loop(0, 6)
                    def _(b):
                        r = pl.ds(pl.multiple_of(h * 384 + b * 64, 64), 64)
                        RS[way, t - 1, r, :] = (RS[way, t - 1, r, :].astype(F32)
                                                + GR[j, r, :].astype(F32)).astype(BF)
                    cp.start()

        @pl.loop(1, 7)
        def _(t):
            step(t, (0, 1))
        step(7, (0,))
        g_wait(z)

    slots = iota((128, 384), 1).astype(F32)
    Q0, Q1 = (slots == t0).astype(BF), (slots == t1).astype(BF)
    qa = (Q0.astype(F32) + Q1.astype(F32)).astype(BF)

    def combine(kind):
        @pl.loop(0, 32)
        def _(e):
            @pl.when(e != me_e)
            def _():
                back_recv(kind, e).wait_recv()
        if kind == 0:
            UO[320:384, :] = jnp.zeros((64, 2048), BF)
            unpack(ro, UO, 0, 10)

            def body(m, carry):
                a0, a1 = carry
                k = pl.ds(pl.multiple_of(m * 256, 256), 256)
                o0, o1 = dot_nn(Q0, UO[:, k]), dot_nn(Q1, UO[:, k])
                mixed[:, k] = (rw[:, 0:1] * o0 + rw[:, 1:2] * o1).astype(BF)
                cf = cot[:, k].astype(F32)
                return (a0 + jnp.sum(cf * o0, axis=1, keepdims=True),
                        a1 + jnp.sum(cf * o1, axis=1, keepdims=True))
            a0, a1 = lax.fori_loop(0, 8, body, (jnp.zeros((128, 1), F32), jnp.zeros((128, 1), F32)))
            rgrad[:, 0:1] = a0
            rgrad[:, 1:2] = a1
        else:
            UG[320:384, :] = jnp.zeros((64, 2048), BF)
            unpack(rg, UG, 0, 10)

            @pl.loop(0, 8)
            def _(m):
                k = pl.ds(pl.multiple_of(m * 256, 256), 256)
                gtok[:, k] = dot_nn(qa, UG[:, k]).astype(BF)

    @on_core(0)
    def _():
        for half in range(2):
            phase_a(half)
            phase_b(half)
        gradients()

    @on_core(1)
    def _():
        phase_a(0)
        phase_a(1)
        gradients()
        phase_b(0)
        phase_b(1)
        reduce_z()

    combine(0)
    combine(1)

    @on_core(0)
    def _():
        @pl.loop(0, 16)
        def _(j):
            g_wait(j)

        @pl.loop(0, 12)
        def _(b):
            r = pl.ds(pl.multiple_of(b * 64, 64), 64)
            acc = GR[0, r, :].astype(F32)
            for i in range(1, 16):
                acc = acc + GR[i, r, :].astype(F32)
            gdown[r, :] = acc

    @on_core(1)
    def _():
        for h in range(2):
            hop(0, 7, h, True)[1].wait_recv()
            hop(1, 6, h, True)[1].wait_recv()

        @pl.loop(0, 12)
        def _(b):
            r = pl.ds(pl.multiple_of(b * 64, 64), 64)
            gdown[r, :] = (GR[z, r, :].astype(F32) + RS[0, 7, r, :].astype(F32)) + RS[1, 6, r, :].astype(F32)

    for i in range(15):
        w_copy(0, i, 0, 384).wait_send()
        g_copy(i, 0, 768).wait_send()
    for kind in range(2):
        @on_core(0)
        def _():
            tok(kind, 0, 1).wait_send()
            back(kind, 0, 1).wait_send()

        @on_core(1)
        def _():
            tok(kind, 0, 0).wait_send()
            back(kind, 0, 0).wait_send()

        @pl.loop(1, 16)
        def _(pos):
            for h in range(2):
                tok(kind, pos, h).wait_send()
                back(kind, pos, h).wait_send()

    @on_core(1)
    def _():
        for way in range(2):
            @pl.loop(0, 7)
            def _(t):
                for h in range(2):
                    ring(way, t, h).wait_send()
            ring(way, 7, way).wait_send()
            for h in range(2):
                hop(way, 0, h, True)[1].wait_send()

            @pl.loop(1, 8 - way)
            def _(t):
                for h in range(2):
                    hop(way, t, h, True)[1].wait_send()


def shards(tokens, cotangent, routes, route_weight, w_gate, w_up, w_down):
    rows, width = tokens.shape
    ff = w_gate.shape[2]
    part = w_gate.shape[1]
    tile = lambda: pltpu.VMEM((320, 16, 128), BF)
    flat = lambda n, w: pltpu.VMEM((n, w), BF)
    dma = pltpu.SemaphoreType.DMA
    out = pl.pallas_call(
        kernel,
        out_shape=(
            jax.ShapeDtypeStruct((rows, width), BF),
            jax.ShapeDtypeStruct((rows, width), BF),
            jax.ShapeDtypeStruct((rows, 2), F32),
            jax.ShapeDtypeStruct((ff, part), F32),
        ),
        in_specs=[pl.BlockSpec(memory_space=pltpu.VMEM)] * 7,
        out_specs=[pl.BlockSpec(memory_space=pltpu.VMEM)] * 4,
        scratch_shapes=[
            pltpu.VMEM((16, 384, 768), BF), pltpu.VMEM((16, 384, 768), BF),
            tile(), tile(), tile(), tile(),
            flat(320, 2048), flat(320, 2048),
            flat(320, 768), flat(320, 768), flat(320, 768),
            flat(320, 2048), flat(320, 2048),
            tile(), tile(), tile(), tile(),
            flat(384, 2048), flat(384, 2048),
            pltpu.VMEM((16, 768, 128), BF), pltpu.VMEM((16, 768, 128), BF),
            pltpu.VMEM((2, 8, 768, 128), BF),
            flat(256, 256),
            dma((15,)), dma((15,)), dma((2, 8, 2)), dma((2, 8, 2)),
            dma((2, 32)), dma((2, 32)), dma((2, 32)), dma((2, 32)),
            dma((15,)), dma((16,)), dma((2, 8, 2)), dma((2, 8, 2)),
        ],
        compiler_params=pltpu.CompilerParams(
            collective_id=0, has_side_effects=True, vmem_limit_bytes=60 * 2**20),
    )(routes, route_weight, tokens, cotangent, w_gate[0], w_up[0], w_down[0])
    mixed, gtok, rgrad, gdown = out
    return (mixed, gtok, rgrad, gdown[None])


def solution(mesh):
    in_specs = (
        P(("dp", "expert"), None),
        P(("dp", "expert"), None),
        P(("dp", "expert"), None),
        P(("dp", "expert"), None),
        P("expert", "dp", None),
        P("expert", "dp", None),
        P("expert", None, "dp"),
    )
    out_specs = (
        P(("dp", "expert"), None),
        P(("dp", "expert"), None),
        P(("dp", "expert"), None),
        P("expert", None, "dp"),
    )
    return jax.shard_map(shards, mesh=mesh, in_specs=in_specs, out_specs=out_specs, check_vma=False)
```

```python
import functools
import jax
import jax.numpy as jnp
from jax import lax
from jax.experimental import pallas as pl
from jax.experimental.pallas import tpu as pltpu
from jax.sharding import PartitionSpec as P

CAP = 10
BF = jnp.bfloat16
F32 = jnp.float32
PLANE = [(1, 0), (0, 1), (3, 0), (0, 3), (2, 0), (0, 2), (1, 1), (3, 3),
         (1, 3), (3, 1), (2, 1), (1, 2), (2, 3), (3, 2), (2, 2)]


def dot_nn(a, b):
    return lax.dot_general(a, b, (((1,), (0,)), ((), ())), preferred_element_type=F32)


def dot_nt(a, b):
    return lax.dot_general(a, b, (((1,), (1,)), ((), ())), preferred_element_type=F32)


def iota(shape, dim):
    return lax.broadcasted_iota(jnp.int32, shape, dim)


def kernel(routes, rw, x, cot, wg, wu, wd, mixed, gtok, rgrad, gdown,
           W, WZ, sx, sc, rx, rc, RX, RC, H, GG, GU, OO, GP, po, pg, ro, rg, UO, UG, GT, GR, RS, S,
           wss, wrs, zss, zrs, tss, trs, bss, brs, gss, grs, rss, rrs, go):
    g = lax.axis_index("dp")
    s = lax.axis_index("expert")
    z, c = s // 2, lax.rem(s, 2)
    px, py = lax.rem(g, 4), g // 4
    me_e = jnp.where(c == 0, 2 * z, 2 * g + 1)

    def on_core(n):
        return pl.when(c == n)

    def plane(d):
        return lax.rem(py + d[1], 4) * 4 + lax.rem(px + d[0], 4)

    def dz(pos):
        return jnp.where(lax.rem(pos, 2) == 1, (pos + 1) // 2, lax.rem(16 - pos // 2, 16))

    def up_z(t):
        return lax.rem(z + t + 16, 16)

    bar = pltpu.get_barrier_semaphore()

    @pl.loop(1, 32)
    def _(d):
        pl.semaphore_signal(bar, inc=1, device_id=(g, lax.rem(s + d, 32)))

    @pl.loop(1, 16)
    def _(d):
        pl.semaphore_signal(bar, inc=1, device_id=(lax.rem(g + d, 16), 2 * z))
        pl.semaphore_signal(bar, inc=1, device_id=(lax.rem(g + d, 16), 2 * z + 1))

    eye = (iota((128, 128), 0) == iota((128, 128), 1))
    down_rows = dot_nt(eye.astype(BF), wd[...]).astype(BF)

    @on_core(0)
    def _():
        W[g, 0:128] = wg[...]
        W[g, 128:256] = wu[...]
        W[g, 256:384] = down_rows

    @on_core(1)
    def _():
        WZ[z, 0:128] = wg[...]
        WZ[z, 128:256] = wu[...]
        WZ[z, 256:384] = down_rows

    pl.semaphore_wait(bar, 31 + 30)

    def w_copy(core, i, r, n):
        p = plane(PLANE[i])
        src = W.at[g, pl.ds(r, n)] if core == 0 else WZ.at[p, pl.ds(r, n)]
        return pltpu.make_async_remote_copy(
            src, W.at[g, pl.ds(r, n)], wss.at[i], wrs.at[i], device_id=(p, s))

    def ring(way, t, h):
        to = up_z(1 - 2 * way)
        sl = lax.rem(z + 16 + (t if way else -t), 16)
        r = pl.ds(h * 64, 64)
        return pltpu.make_async_remote_copy(
            WZ.at[sl, r], WZ.at[sl, r], zss.at[way, t, h], zrs.at[way, t, h],
            device_id=(g, 2 * to + 1))

    def relay(t, last):
        for h in range(6):
            for way in range(2):
                ring(way, t - 1, h).wait_recv()
                if not last or h // 3 == way:
                    ring(way, t, h).start()

    @on_core(0)
    def _():
        @pl.loop(0, 12)
        def _(p):
            for i in range(15):
                w_copy(0, i, p * 32, 32).start()

    @on_core(1)
    def _():
        for h in range(6):
            for way in range(2):
                ring(way, 0, h).start()

    lanes = iota((128, 128), 1)

    def column(row):
        return jnp.sum(jnp.where(eye, row, 0.0), axis=1, keepdims=True)

    def row(col):
        return jnp.sum(jnp.where(eye, col, 0.0), axis=0, keepdims=True)

    w0, w1 = column(rw[0:1, :]), column(rw[1:2, :])
    e0, e1 = column(routes[0:1, :].astype(F32)), column(routes[1:2, :].astype(F32))
    r0, r1 = e0.astype(jnp.int32), e1.astype(jnp.int32)
    h0, h1 = (lanes == r0), (lanes == r1)
    named = (h0.astype(F32) + h1.astype(F32)).astype(BF)
    before = (iota((128, 128), 0) > lanes).astype(BF)
    count = dot_nn(before, named)
    t0 = e0 * CAP + jnp.sum(jnp.where(h0, count, 0.0), axis=1, keepdims=True)
    t1 = e1 * CAP + jnp.sum(jnp.where(h1, count, 0.0), axis=1, keepdims=True)
    u0, u1 = row(t0), row(t1)
    slots = iota((384, 128), 0).astype(F32)
    P0, P1 = (slots == u0).astype(BF), (slots == u1).astype(BF)

    S[...] = (iota((256, 256), 1) == lax.rem(iota((256, 256), 0), 16) * 16
              + iota((256, 256), 0) // 16).astype(BF)

    def pack(src, dst, lo, n):
        @pl.loop(0, n)
        def _(q):
            r = pl.multiple_of(lo + q * 32, 32)
            a = src[pl.ds(r, 32), :]
            cols = [jnp.concatenate([a[h * 16:h * 16 + 16, k * 128:k * 128 + 128] for k in range(16)], axis=0)
                    for h in range(2)]
            o = dot_nn(S[...], jnp.concatenate(cols, axis=1)).astype(BF)
            dst[pl.ds(r, 16)] = o[:, :128].reshape(16, 16, 128)
            dst[pl.ds(r + 16, 16)] = o[:, 128:].reshape(16, 16, 128)

    def unpack(src, dst, lo, n):
        @pl.loop(0, n)
        def _(q):
            r = pl.multiple_of(lo + q * 32, 32)
            a = src[pl.ds(r, 32)].reshape(512, 128)
            o = dot_nn(S[...], jnp.concatenate([a[:256], a[256:]], axis=1)).astype(BF)
            for h in range(2):
                dst[pl.ds(r + h * 16, 16), :] = jnp.concatenate(
                    [o[k * 16:k * 16 + 16, h * 128:h * 128 + 128] for k in range(16)], axis=1)

    def chip(pos, sign):
        dx, dy = lax.rem(pos, 4), pos // 4
        return lax.rem(py + sign * dy + 4, 4) * 4 + lax.rem(px + sign * dx + 4, 4)

    def tok(kind, pos, hc):
        src, dst = ((sx, rx), (sc, rc))[kind]
        if hc == 0:
            e = lax.rem(z + dz(pos), 16) * 2
            dev = (g, e)
        else:
            j = chip(pos, 1)
            e = 2 * j + 1
            dev = (j, 2 * z + 1)
        return pltpu.make_async_remote_copy(
            src.at[pl.ds(e * CAP, CAP)], dst.at[pl.ds((2 * pos + c) * CAP, CAP)],
            tss.at[kind, 2 * pos + hc], trs.at[kind, 2 * pos + c], device_id=dev)

    def tok_recv(kind, q):
        src, dst = ((sx, rx), (sc, rc))[kind]
        return pltpu.make_async_remote_copy(
            src.at[pl.ds(0, CAP)], dst.at[pl.ds(q * CAP, CAP)],
            tss.at[kind, q], trs.at[kind, q], device_id=(g, s + 1 - 2 * c))

    def send_tokens(kind, hc, first=0):
        if first == 0:
            @on_core(1 - hc)
            def _():
                tok(kind, 0, hc).start()

        @pl.loop(max(first, 1), 16)
        def _(pos):
            tok(kind, pos, hc).start()

    def send_token_pair(kind, p):
        tok(kind, 2 * p, 0).start()
        tok(kind, 2 * p + 1, 0).start()

    def keep(kind):
        src, dst = ((sx, rx), (sc, rc))[kind]
        dst[pl.ds(c * CAP, CAP)] = src[pl.ds(me_e * CAP, CAP)]

    pa = (P0.astype(F32) + P1.astype(F32)).astype(BF)

    @pl.loop(0, 8)
    def _(m):
        k = pl.ds(pl.multiple_of(m * 256, 256), 256)
        UO[:, k] = dot_nn(pa, x[:, k]).astype(BF)
    pack(UO, sx, 0, 10)
    keep(0)
    send_tokens(0, 1)

    @on_core(1)
    def _():
        relay(1, False)

    @pl.loop(0, 8)
    def _(m):
        k = pl.ds(pl.multiple_of(m * 256, 256), 256)
        cf = cot[:, k].astype(F32)
        v0 = (cf * w0).astype(BF)
        v1 = (cf * w1).astype(BF)
        UG[:, k] = (dot_nn(P0, v0) + dot_nn(P1, v1)).astype(BF)
    pack(UG, sc, 0, 10)
    keep(1)
    send_tokens(1, 1)

    @on_core(0)
    def _():
        pl.semaphore_wait(go, 1)
        send_tokens(0, 0)
        send_tokens(1, 0)

    @on_core(1)
    def _():
        @pl.loop(2, 6)
        def _(t):
            relay(t, False)
        pl.semaphore_signal(go, inc=1, device_id=(g, 2 * z))
        relay(6, False)
        relay(7, True)
        far = lax.rem(z + 8, 16)

        @pl.loop(0, 6)
        def _(p):
            for i in range(15):
                @pl.when(plane(PLANE[i]) != far)
                def _():
                    w_copy(1, i, p * 64, 64).start()
            for kind in range(2):
                send_token_pair(kind, p)
        for way in range(2):
            for h in range(3):
                ring(way, 7, way * 3 + h).wait_recv()
        for i in range(15):
            @pl.when(plane(PLANE[i]) == far)
            def _():
                @pl.loop(0, 6)
                def _(p):
                    w_copy(1, i, p * 64, 64).start()
        for kind in range(2):
            send_tokens(kind, 0, 12)
        W[g] = WZ[g]

    for i in range(15):
        w_copy(0, i, 0, 384).wait_recv()

    def back(kind, pos, cc):
        src, dst = ((po, ro), (pg, rg))[kind]
        dev = (jnp.where(c == 0, g, chip(pos, -1)),
               jnp.where(c == 0, lax.rem(z + 16 - dz(pos), 16), z) * 2 + cc)
        return pltpu.make_async_remote_copy(
            src.at[pl.ds((2 * pos + cc) * CAP, CAP)], dst.at[pl.ds(me_e * CAP, CAP)],
            bss.at[kind, 2 * pos + cc], brs.at[kind, me_e], device_id=dev)

    def back_recv(kind, e):
        src, dst = ((po, ro), (pg, rg))[kind]
        return pltpu.make_async_remote_copy(
            src.at[pl.ds(0, CAP)], dst.at[pl.ds(e * CAP, CAP)],
            bss.at[kind, e], brs.at[kind, e], device_id=(g, s + 1 - 2 * c))

    def phase_a(half):
        for kind in range(2):
            if half == 0:
                tok_recv(kind, 1 - c).wait_recv()

            @pl.loop(half * 16 + (2 if half == 0 else 0), half * 16 + 16)
            def _(q):
                tok_recv(kind, q).wait_recv()
        lo = half * 160
        unpack(rx, RX, lo, 5)
        unpack(rc, RC, lo, 5)
        rows = pl.ds(lo, 160)

        @pl.loop(0, 3)
        def _(n):
            k = pl.ds(pl.multiple_of(n * 256, 256), 256)
            xs, cs = RX[rows, :], RC[rows, :]
            gate = dot_nn(xs, W[:, 0:128, k].reshape(2048, 256))
            up = dot_nn(xs, W[:, 128:256, k].reshape(2048, 256))
            gh = dot_nn(cs, W[:, 256:384, k].reshape(2048, 256))
            sig = jax.nn.sigmoid(gate)
            act = gate * sig
            H[rows, k] = (act * up).astype(BF)
            GG[rows, k] = (gh * up * sig * (1.0 + gate * (1.0 - sig))).astype(BF)
            GU[rows, k] = (gh * act).astype(BF)

    def phase_b(half):
        lo = half * 160
        rows = pl.ds(lo, 160)

        @pl.loop(0, 8)
        def _(m):
            k = pl.ds(pl.multiple_of(m * 256, 256), 256)
            j = pl.ds(2 * m, 2)
            OO[rows, k] = dot_nt(H[rows, :], W[j, 256:384, :].reshape(256, 768)).astype(BF)
            GP[rows, k] = (dot_nt(GG[rows, :], W[j, 0:128, :].reshape(256, 768))
                           + dot_nt(GU[rows, :], W[j, 128:256, :].reshape(256, 768))).astype(BF)
        for kind in range(2):
            src, dst, flat = ((po, ro, OO), (pg, rg, GP))[kind]
            pack(flat, src, lo, 5)
            if half == 0:
                back(kind, 0, 1 - c).start()
                dst[pl.ds(me_e * CAP, CAP)] = src[pl.ds(c * CAP, CAP)]

            @pl.loop(half * 8 + (1 if half == 0 else 0), half * 8 + 8)
            def _(pos):
                back(kind, pos, 0).start()
                back(kind, pos, 1).start()

    def g_copy(i, r, n):
        p = plane(PLANE[i])
        return pltpu.make_async_remote_copy(
            GT.at[p, pl.ds(r, n)], GR.at[g, pl.ds(r, n)], gss.at[i], grs.at[g], device_id=(p, s))

    def g_recv(j):
        return pltpu.make_async_remote_copy(
            GT.at[j], GR.at[j], gss.at[0], grs.at[j], device_id=(g, s + 1 - 2 * c))

    def gradients():
        HT = jnp.transpose(H[...])

        @pl.loop(0, 8)
        def _(m):
            k = pl.ds(pl.multiple_of(m * 256, 256), 256)
            t = dot_nn(HT, RC[:, k]).astype(BF)
            GT[2 * m] = t[:, :128]
            GT[2 * m + 1] = t[:, 128:]

        @pl.loop(0, 4)
        def _(p):
            for i in range(15):
                g_copy(i, p * 192, 192).start()
        GR[g] = GT[g]

    def hop(way, t, h, first=False):
        to = up_z(1 - 2 * way)
        j = lax.rem(z + 16 + (t - 7 if way else 8 - t), 16)
        r = pl.ds(h * 384, 384)
        src = GR.at[j, r] if first else RS.at[way, t - 1, r]
        return j, pltpu.make_async_remote_copy(
            src, RS.at[way, t, r], rss.at[way, t, h], rrs.at[way, t, h], device_id=(g, 2 * to + 1))

    def g_wait(j):
        @pl.when(j != g)
        def _():
            g_recv(j).wait_recv()

    def reduce_z():
        for way in range(2):
            for h in range(2):
                j, cp = hop(way, 0, h, True)
                if h == 0:
                    g_wait(j)
                cp.start()

        def step(t, ways):
            for h in range(2):
                for way in ways:
                    j, cp = hop(way, t, h)
                    if h == 0:
                        g_wait(j)
                    hop(way, t - 1, h, True)[1].wait_recv()

                    @pl.loop(0, 6)
                    def _(b):
                        r = pl.ds(pl.multiple_of(h * 384 + b * 64, 64), 64)
                        RS[way, t - 1, r, :] = (RS[way, t - 1, r, :].astype(F32)
                                                + GR[j, r, :].astype(F32)).astype(BF)
                    cp.start()

        @pl.loop(1, 7)
        def _(t):
            step(t, (0, 1))
        step(7, (0,))
        g_wait(z)

    slots = iota((128, 384), 1).astype(F32)
    Q0, Q1 = (slots == t0).astype(BF), (slots == t1).astype(BF)
    qa = (Q0.astype(F32) + Q1.astype(F32)).astype(BF)

    def combine(kind):
        @pl.loop(0, 32)
        def _(e):
            @pl.when(e != me_e)
            def _():
                back_recv(kind, e).wait_recv()
        if kind == 0:
            UO[320:384, :] = jnp.zeros((64, 2048), BF)
            unpack(ro, UO, 0, 10)

            def body(m, carry):
                a0, a1 = carry
                k = pl.ds(pl.multiple_of(m * 256, 256), 256)
                o0, o1 = dot_nn(Q0, UO[:, k]), dot_nn(Q1, UO[:, k])
                mixed[:, k] = (w0 * o0 + w1 * o1).astype(BF)
                cf = cot[:, k].astype(F32)
                return (a0 + jnp.sum(cf * o0, axis=1, keepdims=True),
                        a1 + jnp.sum(cf * o1, axis=1, keepdims=True))
            a0, a1 = lax.fori_loop(0, 8, body, (jnp.zeros((128, 1), F32), jnp.zeros((128, 1), F32)))
            rgrad[0:1, :] = row(a0)
            rgrad[1:2, :] = row(a1)
        else:
            UG[320:384, :] = jnp.zeros((64, 2048), BF)
            unpack(rg, UG, 0, 10)

            @pl.loop(0, 8)
            def _(m):
                k = pl.ds(pl.multiple_of(m * 256, 256), 256)
                gtok[:, k] = dot_nn(qa, UG[:, k]).astype(BF)

    @on_core(0)
    def _():
        for half in range(2):
            phase_a(half)
            phase_b(half)
        gradients()

    @on_core(1)
    def _():
        phase_a(0)
        phase_a(1)
        gradients()
        phase_b(0)
        phase_b(1)
        reduce_z()

    combine(0)
    combine(1)

    @on_core(0)
    def _():
        @pl.loop(0, 16)
        def _(j):
            g_wait(j)

        @pl.loop(0, 12)
        def _(b):
            r = pl.ds(pl.multiple_of(b * 64, 64), 64)
            acc = GR[0, r, :].astype(F32)
            for i in range(1, 16):
                acc = acc + GR[i, r, :].astype(F32)
            gdown[r, :] = acc

    @on_core(1)
    def _():
        for h in range(2):
            hop(0, 7, h, True)[1].wait_recv()
            hop(1, 6, h, True)[1].wait_recv()

        @pl.loop(0, 12)
        def _(b):
            r = pl.ds(pl.multiple_of(b * 64, 64), 64)
            gdown[r, :] = (GR[z, r, :].astype(F32) + RS[0, 7, r, :].astype(F32)) + RS[1, 6, r, :].astype(F32)

    for i in range(15):
        w_copy(0, i, 0, 384).wait_send()
        g_copy(i, 0, 768).wait_send()
    for kind in range(2):
        @on_core(0)
        def _():
            tok(kind, 0, 1).wait_send()
            back(kind, 0, 1).wait_send()

        @on_core(1)
        def _():
            tok(kind, 0, 0).wait_send()
            back(kind, 0, 0).wait_send()

        @pl.loop(1, 16)
        def _(pos):
            for h in range(2):
                tok(kind, pos, h).wait_send()
                back(kind, pos, h).wait_send()

    @on_core(1)
    def _():
        for way in range(2):
            @pl.loop(0, 7)
            def _(t):
                for h in range(6):
                    ring(way, t, h).wait_send()
            for h in range(3):
                ring(way, 7, way * 3 + h).wait_send()
            for h in range(2):
                hop(way, 0, h, True)[1].wait_send()

            @pl.loop(1, 8 - way)
            def _(t):
                for h in range(2):
                    hop(way, t, h, True)[1].wait_send()


def shards(tokens, cotangent, routes, route_weight, w_gate, w_up, w_down):
    rows, width = tokens.shape
    ff = w_gate.shape[2]
    part = w_gate.shape[1]
    tile = lambda: pltpu.VMEM((320, 16, 128), BF)
    flat = lambda n, w: pltpu.VMEM((n, w), BF)
    dma = pltpu.SemaphoreType.DMA
    out = pl.pallas_call(
        kernel,
        out_shape=(
            jax.ShapeDtypeStruct((rows, width), BF),
            jax.ShapeDtypeStruct((rows, width), BF),
            jax.ShapeDtypeStruct((2, rows), F32),
            jax.ShapeDtypeStruct((ff, part), F32),
        ),
        in_specs=[pl.BlockSpec(memory_space=pltpu.VMEM)] * 7,
        out_specs=[pl.BlockSpec(memory_space=pltpu.VMEM)] * 4,
        scratch_shapes=[
            pltpu.VMEM((16, 384, 768), BF), pltpu.VMEM((16, 384, 768), BF),
            tile(), tile(), tile(), tile(),
            flat(320, 2048), flat(320, 2048),
            flat(320, 768), flat(320, 768), flat(320, 768),
            flat(320, 2048), flat(320, 2048),
            tile(), tile(), tile(), tile(),
            flat(384, 2048), flat(384, 2048),
            pltpu.VMEM((16, 768, 128), BF), pltpu.VMEM((16, 768, 128), BF),
            pltpu.VMEM((2, 8, 768, 128), BF),
            flat(256, 256),
            dma((15,)), dma((15,)), dma((2, 8, 6)), dma((2, 8, 6)),
            dma((2, 32)), dma((2, 32)), dma((2, 32)), dma((2, 32)),
            dma((15,)), dma((16,)), dma((2, 8, 2)), dma((2, 8, 2)),
            pltpu.SemaphoreType.REGULAR,
        ],
        compiler_params=pltpu.CompilerParams(
            collective_id=0, has_side_effects=True, vmem_limit_bytes=60 * 2**20),
    )(routes.T, route_weight.T, tokens, cotangent, w_gate[0], w_up[0], w_down[0])
    mixed, gtok, rgrad, gdown = out
    return (mixed, gtok, rgrad.T, gdown[None])


def solution(mesh):
    in_specs = (
        P(("dp", "expert"), None),
        P(("dp", "expert"), None),
        P(("dp", "expert"), None),
        P(("dp", "expert"), None),
        P("expert", "dp", None),
        P("expert", "dp", None),
        P("expert", None, "dp"),
    )
    out_specs = (
        P(("dp", "expert"), None),
        P(("dp", "expert"), None),
        P(("dp", "expert"), None),
        P("expert", None, "dp"),
    )
    return jax.shard_map(shards, mesh=mesh, in_specs=in_specs, out_specs=out_specs, check_vma=False)
```

```python
import functools
import jax
import jax.numpy as jnp
from jax import lax
from jax.experimental import pallas as pl
from jax.experimental.pallas import tpu as pltpu
from jax.sharding import PartitionSpec as P

CAP = 10
BF = jnp.bfloat16
F32 = jnp.float32
PLANE = [(1, 0), (0, 1), (3, 0), (0, 3), (2, 0), (0, 2), (1, 1), (3, 3),
         (1, 3), (3, 1), (2, 1), (1, 2), (2, 3), (3, 2), (2, 2)]


def dot_nn(a, b):
    return lax.dot_general(a, b, (((1,), (0,)), ((), ())), preferred_element_type=F32)


def dot_nt(a, b):
    return lax.dot_general(a, b, (((1,), (1,)), ((), ())), preferred_element_type=F32)


def iota(shape, dim):
    return lax.broadcasted_iota(jnp.int32, shape, dim)


def kernel(routes, rw, x, cot, wg, wu, wd, mixed, gtok, rgrad, gdown,
           W, WZ, sx, sc, rx, rc, RX, RC, H, GG, GU, OO, GP, po, pg, ro, rg, UO, UG, GT, GR, RS, S,
           wss, wrs, zss, zrs, tss, trs, bss, brs, gss, grs, rss, rrs):
    g = lax.axis_index("dp")
    s = lax.axis_index("expert")
    z, c = s // 2, lax.rem(s, 2)
    px, py = lax.rem(g, 4), g // 4
    me_e = jnp.where(c == 0, 2 * z, 2 * g + 1)

    def on_core(n):
        return pl.when(c == n)

    def plane(d):
        return lax.rem(py + d[1], 4) * 4 + lax.rem(px + d[0], 4)

    def dz(pos):
        return jnp.where(lax.rem(pos, 2) == 1, (pos + 1) // 2, lax.rem(16 - pos // 2, 16))

    def up_z(t):
        return lax.rem(z + t + 16, 16)

    bar = pltpu.get_barrier_semaphore()

    @pl.loop(1, 32)
    def _(d):
        pl.semaphore_signal(bar, inc=1, device_id=(g, lax.rem(s + d, 32)))

    @pl.loop(1, 16)
    def _(d):
        pl.semaphore_signal(bar, inc=1, device_id=(lax.rem(g + d, 16), 2 * z))
        pl.semaphore_signal(bar, inc=1, device_id=(lax.rem(g + d, 16), 2 * z + 1))

    eye = (iota((128, 128), 0) == iota((128, 128), 1))
    down_rows = dot_nt(eye.astype(BF), wd[...]).astype(BF)

    @on_core(0)
    def _():
        W[g, 0:128] = wg[...]
        W[g, 128:256] = wu[...]
        W[g, 256:384] = down_rows

    @on_core(1)
    def _():
        WZ[z, 0:128] = wg[...]
        WZ[z, 128:256] = wu[...]
        WZ[z, 256:384] = down_rows

    pl.semaphore_wait(bar, 31 + 30)

    def w_copy(core, i, r, n):
        p = plane(PLANE[i])
        src = W.at[g, pl.ds(r, n)] if core == 0 else WZ.at[p, pl.ds(r, n)]
        return pltpu.make_async_remote_copy(
            src, W.at[g, pl.ds(r, n)], wss.at[i], wrs.at[i], device_id=(p, s))

    def ring(way, t, h):
        to = up_z(1 - 2 * way)
        sl = lax.rem(z + 16 + (t if way else -t), 16)
        r = pl.ds(h * 192, 192)
        return pltpu.make_async_remote_copy(
            WZ.at[sl, r], WZ.at[sl, r], zss.at[way, t, h], zrs.at[way, t, h],
            device_id=(g, 2 * to + 1))

    def relay(t, last):
        for h in range(2):
            for way in range(2):
                ring(way, t - 1, h).wait_recv()
                if not last or h == way:
                    ring(way, t, h).start()

    @on_core(0)
    def _():
        @pl.loop(0, 12)
        def _(p):
            for i in range(15):
                w_copy(0, i, p * 32, 32).start()

    @on_core(1)
    def _():
        for h in range(2):
            for way in range(2):
                ring(way, 0, h).start()

    lanes = iota((128, 128), 1)

    def column(row):
        return jnp.sum(jnp.where(eye, row, 0.0), axis=1, keepdims=True)

    def row(col):
        return jnp.sum(jnp.where(eye, col, 0.0), axis=0, keepdims=True)

    w0, w1 = column(rw[0:1, :]), column(rw[1:2, :])
    e0, e1 = column(routes[0:1, :].astype(F32)), column(routes[1:2, :].astype(F32))
    r0, r1 = e0.astype(jnp.int32), e1.astype(jnp.int32)
    h0, h1 = (lanes == r0), (lanes == r1)
    named = (h0.astype(F32) + h1.astype(F32)).astype(BF)
    before = (iota((128, 128), 0) > lanes).astype(BF)
    count = dot_nn(before, named)
    t0 = e0 * CAP + jnp.sum(jnp.where(h0, count, 0.0), axis=1, keepdims=True)
    t1 = e1 * CAP + jnp.sum(jnp.where(h1, count, 0.0), axis=1, keepdims=True)
    u0, u1 = row(t0), row(t1)
    slots = iota((384, 128), 0).astype(F32)
    P0, P1 = (slots == u0).astype(BF), (slots == u1).astype(BF)

    S[...] = (iota((256, 256), 1) == lax.rem(iota((256, 256), 0), 16) * 16
              + iota((256, 256), 0) // 16).astype(BF)

    def pack(src, dst, lo, n):
        @pl.loop(0, n)
        def _(q):
            r = pl.multiple_of(lo + q * 32, 32)
            a = src[pl.ds(r, 32), :]
            cols = [jnp.concatenate([a[h * 16:h * 16 + 16, k * 128:k * 128 + 128] for k in range(16)], axis=0)
                    for h in range(2)]
            o = dot_nn(S[...], jnp.concatenate(cols, axis=1)).astype(BF)
            dst[pl.ds(r, 16)] = o[:, :128].reshape(16, 16, 128)
            dst[pl.ds(r + 16, 16)] = o[:, 128:].reshape(16, 16, 128)

    def unpack(src, dst, lo, n):
        @pl.loop(0, n)
        def _(q):
            r = pl.multiple_of(lo + q * 32, 32)
            a = src[pl.ds(r, 32)].reshape(512, 128)
            o = dot_nn(S[...], jnp.concatenate([a[:256], a[256:]], axis=1)).astype(BF)
            for h in range(2):
                dst[pl.ds(r + h * 16, 16), :] = jnp.concatenate(
                    [o[k * 16:k * 16 + 16, h * 128:h * 128 + 128] for k in range(16)], axis=1)

    def chip(pos, sign):
        dx, dy = lax.rem(pos, 4), pos // 4
        return lax.rem(py + sign * dy + 4, 4) * 4 + lax.rem(px + sign * dx + 4, 4)

    def tok(kind, pos, hc):
        src, dst = ((sx, rx), (sc, rc))[kind]
        if hc == 0:
            e = lax.rem(z + dz(pos), 16) * 2
            dev = (g, e)
        else:
            j = chip(pos, 1)
            e = 2 * j + 1
            dev = (j, 2 * z + 1)
        return pltpu.make_async_remote_copy(
            src.at[pl.ds(e * CAP, CAP)], dst.at[pl.ds((16 * c + pos) * CAP, CAP)],
            tss.at[kind, 16 * hc + pos], trs.at[kind, 16 * c + pos], device_id=dev)

    def tok_recv(kind, q):
        src, dst = ((sx, rx), (sc, rc))[kind]
        return pltpu.make_async_remote_copy(
            src.at[pl.ds(0, CAP)], dst.at[pl.ds(q * CAP, CAP)],
            tss.at[kind, q], trs.at[kind, q], device_id=(g, s + 1 - 2 * c))

    def send_tokens(kind, hc, first=0):
        if first == 0:
            @on_core(1 - hc)
            def _():
                tok(kind, 0, hc).start()

        @pl.loop(max(first, 1), 16)
        def _(pos):
            tok(kind, pos, hc).start()

    def keep(kind):
        src, dst = ((sx, rx), (sc, rc))[kind]
        dst[pl.ds(16 * c * CAP, CAP)] = src[pl.ds(me_e * CAP, CAP)]

    pa = (P0.astype(F32) + P1.astype(F32)).astype(BF)

    @pl.loop(0, 8)
    def _(m):
        k = pl.ds(pl.multiple_of(m * 256, 256), 256)
        UO[:, k] = dot_nn(pa, x[:, k]).astype(BF)
    pack(UO, sx, 0, 10)
    keep(0)
    send_tokens(0, 1)

    @on_core(0)
    def _():
        send_tokens(0, 0)

    @on_core(1)
    def _():
        relay(1, False)

    @pl.loop(0, 8)
    def _(m):
        k = pl.ds(pl.multiple_of(m * 256, 256), 256)
        cf = cot[:, k].astype(F32)
        v0 = (cf * w0).astype(BF)
        v1 = (cf * w1).astype(BF)
        UG[:, k] = (dot_nn(P0, v0) + dot_nn(P1, v1)).astype(BF)
    pack(UG, sc, 0, 10)
    keep(1)
    send_tokens(1, 1)

    @on_core(0)
    def _():
        send_tokens(1, 0)

    @on_core(1)
    def _():
        @pl.loop(2, 7)
        def _(t):
            relay(t, False)
        relay(7, True)
        for way in range(2):
            ring(way, 7, way).wait_recv()
        W[g] = WZ[g]
        for kind in range(2):
            tok(kind, 0, 0).start()

        @pl.loop(0, 12)
        def _(p):
            for i in range(15):
                w_copy(1, i, p * 32, 32).start()
            for kind in range(2):
                tok(kind, p + 1, 0).start()
        for kind in range(2):
            send_tokens(kind, 0, 13)

    for i in range(15):
        w_copy(0, i, 0, 384).wait_recv()

    def back(kind, pos, cc):
        src, dst = ((po, ro), (pg, rg))[kind]
        dev = (jnp.where(c == 0, g, chip(pos, -1)),
               jnp.where(c == 0, lax.rem(z + 16 - dz(pos), 16), z) * 2 + cc)
        return pltpu.make_async_remote_copy(
            src.at[pl.ds((16 * cc + pos) * CAP, CAP)], dst.at[pl.ds(me_e * CAP, CAP)],
            bss.at[kind, 16 * cc + pos], brs.at[kind, me_e], device_id=dev)

    def back_recv(kind, e):
        src, dst = ((po, ro), (pg, rg))[kind]
        return pltpu.make_async_remote_copy(
            src.at[pl.ds(0, CAP)], dst.at[pl.ds(e * CAP, CAP)],
            bss.at[kind, e], brs.at[kind, e], device_id=(g, s + 1 - 2 * c))

    def phase_a(half, own):
        for kind in range(2):
            @pl.loop(half * 16 + (1 if half == own else 0), half * 16 + 16)
            def _(q):
                tok_recv(kind, q).wait_recv()
        lo = half * 160
        unpack(rx, RX, lo, 5)
        unpack(rc, RC, lo, 5)
        rows = pl.ds(lo, 160)

        @pl.loop(0, 3)
        def _(n):
            k = pl.ds(pl.multiple_of(n * 256, 256), 256)
            xs, cs = RX[rows, :], RC[rows, :]
            gate = dot_nn(xs, W[:, 0:128, k].reshape(2048, 256))
            up = dot_nn(xs, W[:, 128:256, k].reshape(2048, 256))
            gh = dot_nn(cs, W[:, 256:384, k].reshape(2048, 256))
            sig = jax.nn.sigmoid(gate)
            act = gate * sig
            H[rows, k] = (act * up).astype(BF)
            GG[rows, k] = (gh * up * sig * (1.0 + gate * (1.0 - sig))).astype(BF)
            GU[rows, k] = (gh * act).astype(BF)

    def phase_b(half, own):
        lo = half * 160
        rows = pl.ds(lo, 160)

        @pl.loop(0, 8)
        def _(m):
            k = pl.ds(pl.multiple_of(m * 256, 256), 256)
            j = pl.ds(2 * m, 2)
            OO[rows, k] = dot_nt(H[rows, :], W[j, 256:384, :].reshape(256, 768)).astype(BF)
            GP[rows, k] = (dot_nt(GG[rows, :], W[j, 0:128, :].reshape(256, 768))
                           + dot_nt(GU[rows, :], W[j, 128:256, :].reshape(256, 768))).astype(BF)
        for kind in range(2):
            src, dst, flat = ((po, ro, OO), (pg, rg, GP))[kind]
            pack(flat, src, lo, 5)
            if half == own:
                dst[pl.ds(me_e * CAP, CAP)] = src[pl.ds(16 * own * CAP, CAP)]

            @pl.loop(1 if half == own else 0, 16)
            def _(pos):
                back(kind, pos, half).start()

    def g_copy(i, r, n):
        p = plane(PLANE[i])
        return pltpu.make_async_remote_copy(
            GT.at[p, pl.ds(r, n)], GR.at[g, pl.ds(r, n)], gss.at[i], grs.at[g], device_id=(p, s))

    def g_recv(j):
        return pltpu.make_async_remote_copy(
            GT.at[j], GR.at[j], gss.at[0], grs.at[j], device_id=(g, s + 1 - 2 * c))

    def gradients():
        HT = jnp.transpose(H[...])

        @pl.loop(0, 8)
        def _(m):
            k = pl.ds(pl.multiple_of(m * 256, 256), 256)
            t = dot_nn(HT, RC[:, k]).astype(BF)
            GT[2 * m] = t[:, :128]
            GT[2 * m + 1] = t[:, 128:]

        @pl.loop(0, 4)
        def _(p):
            for i in range(15):
                g_copy(i, p * 192, 192).start()
        GR[g] = GT[g]

    def hop(way, t, h, first=False):
        to = up_z(1 - 2 * way)
        j = lax.rem(z + 16 + (t - 7 if way else 8 - t), 16)
        r = pl.ds(h * 384, 384)
        src = GR.at[j, r] if first else RS.at[way, t - 1, r]
        return j, pltpu.make_async_remote_copy(
            src, RS.at[way, t, r], rss.at[way, t, h], rrs.at[way, t, h], device_id=(g, 2 * to + 1))

    def g_wait(j):
        @pl.when(j != g)
        def _():
            g_recv(j).wait_recv()

    def reduce_z():
        for way in range(2):
            for h in range(2):
                j, cp = hop(way, 0, h, True)
                if h == 0:
                    g_wait(j)
                cp.start()

        def step(t, ways):
            for h in range(2):
                for way in ways:
                    j, cp = hop(way, t, h)
                    if h == 0:
                        g_wait(j)
                    hop(way, t - 1, h, True)[1].wait_recv()

                    @pl.loop(0, 6)
                    def _(b):
                        r = pl.ds(pl.multiple_of(h * 384 + b * 64, 64), 64)
                        RS[way, t - 1, r, :] = (RS[way, t - 1, r, :].astype(F32)
                                                + GR[j, r, :].astype(F32)).astype(BF)
                    cp.start()

        @pl.loop(1, 7)
        def _(t):
            step(t, (0, 1))
        step(7, (0,))
        g_wait(z)

    slots = iota((128, 384), 1).astype(F32)
    Q0, Q1 = (slots == t0).astype(BF), (slots == t1).astype(BF)
    qa = (Q0.astype(F32) + Q1.astype(F32)).astype(BF)

    def combine(kind):
        @pl.loop(0, 32)
        def _(e):
            @pl.when(e != me_e)
            def _():
                back_recv(kind, e).wait_recv()
        if kind == 0:
            UO[320:384, :] = jnp.zeros((64, 2048), BF)
            unpack(ro, UO, 0, 10)

            def body(m, carry):
                a0, a1 = carry
                k = pl.ds(pl.multiple_of(m * 256, 256), 256)
                o0, o1 = dot_nn(Q0, UO[:, k]), dot_nn(Q1, UO[:, k])
                mixed[:, k] = (w0 * o0 + w1 * o1).astype(BF)
                cf = cot[:, k].astype(F32)
                return (a0 + jnp.sum(cf * o0, axis=1, keepdims=True),
                        a1 + jnp.sum(cf * o1, axis=1, keepdims=True))
            a0, a1 = lax.fori_loop(0, 8, body, (jnp.zeros((128, 1), F32), jnp.zeros((128, 1), F32)))
            rgrad[0:1, :] = row(a0)
            rgrad[1:2, :] = row(a1)
        else:
            UG[320:384, :] = jnp.zeros((64, 2048), BF)
            unpack(rg, UG, 0, 10)

            @pl.loop(0, 8)
            def _(m):
                k = pl.ds(pl.multiple_of(m * 256, 256), 256)
                gtok[:, k] = dot_nn(qa, UG[:, k]).astype(BF)

    @on_core(0)
    def _():
        for half in range(2):
            phase_a(half, 0)
            phase_b(half, 0)
        gradients()

    @on_core(1)
    def _():
        phase_a(0, 1)
        phase_a(1, 1)
        gradients()
        phase_b(0, 1)
        phase_b(1, 1)

    combine(0)

    @on_core(1)
    def _():
        reduce_z()

    combine(1)

    @on_core(0)
    def _():
        @pl.loop(0, 16)
        def _(j):
            g_wait(j)

        @pl.loop(0, 12)
        def _(b):
            r = pl.ds(pl.multiple_of(b * 64, 64), 64)
            acc = GR[0, r, :].astype(F32)
            for i in range(1, 16):
                acc = acc + GR[i, r, :].astype(F32)
            gdown[r, :] = acc

    @on_core(1)
    def _():
        for h in range(2):
            hop(0, 7, h, True)[1].wait_recv()
            hop(1, 6, h, True)[1].wait_recv()

        @pl.loop(0, 12)
        def _(b):
            r = pl.ds(pl.multiple_of(b * 64, 64), 64)
            gdown[r, :] = (GR[z, r, :].astype(F32) + RS[0, 7, r, :].astype(F32)) + RS[1, 6, r, :].astype(F32)

    for i in range(15):
        w_copy(0, i, 0, 384).wait_send()
        g_copy(i, 0, 768).wait_send()
    for kind in range(2):
        @on_core(0)
        def _():
            tok(kind, 0, 1).wait_send()
            back(kind, 0, 1).wait_send()

        @on_core(1)
        def _():
            tok(kind, 0, 0).wait_send()
            back(kind, 0, 0).wait_send()

        @pl.loop(1, 16)
        def _(pos):
            for h in range(2):
                tok(kind, pos, h).wait_send()
                back(kind, pos, h).wait_send()

    @on_core(1)
    def _():
        for way in range(2):
            @pl.loop(0, 7)
            def _(t):
                for h in range(2):
                    ring(way, t, h).wait_send()
            ring(way, 7, way).wait_send()
            for h in range(2):
                hop(way, 0, h, True)[1].wait_send()

            @pl.loop(1, 8 - way)
            def _(t):
                for h in range(2):
                    hop(way, t, h, True)[1].wait_send()


def shards(tokens, cotangent, routes, route_weight, w_gate, w_up, w_down):
    rows, width = tokens.shape
    ff = w_gate.shape[2]
    part = w_gate.shape[1]
    tile = lambda: pltpu.VMEM((320, 16, 128), BF)
    flat = lambda n, w: pltpu.VMEM((n, w), BF)
    dma = pltpu.SemaphoreType.DMA
    out = pl.pallas_call(
        kernel,
        out_shape=(
            jax.ShapeDtypeStruct((rows, width), BF),
            jax.ShapeDtypeStruct((rows, width), BF),
            jax.ShapeDtypeStruct((2, rows), F32),
            jax.ShapeDtypeStruct((ff, part), F32),
        ),
        in_specs=[pl.BlockSpec(memory_space=pltpu.VMEM)] * 7,
        out_specs=[pl.BlockSpec(memory_space=pltpu.VMEM)] * 4,
        scratch_shapes=[
            pltpu.VMEM((16, 384, 768), BF), pltpu.VMEM((16, 384, 768), BF),
            tile(), tile(), tile(), tile(),
            flat(320, 2048), flat(320, 2048),
            flat(320, 768), flat(320, 768), flat(320, 768),
            flat(320, 2048), flat(320, 2048),
            tile(), tile(), tile(), tile(),
            flat(384, 2048), flat(384, 2048),
            pltpu.VMEM((16, 768, 128), BF), pltpu.VMEM((16, 768, 128), BF),
            pltpu.VMEM((2, 8, 768, 128), BF),
            flat(256, 256),
            dma((15,)), dma((15,)), dma((2, 8, 2)), dma((2, 8, 2)),
            dma((2, 32)), dma((2, 32)), dma((2, 32)), dma((2, 32)),
            dma((15,)), dma((16,)), dma((2, 8, 2)), dma((2, 8, 2)),
        ],
        compiler_params=pltpu.CompilerParams(
            collective_id=0, has_side_effects=True, vmem_limit_bytes=60 * 2**20),
    )(routes.T, route_weight.T, tokens, cotangent, w_gate[0], w_up[0], w_down[0])
    mixed, gtok, rgrad, gdown = out
    return (mixed, gtok, rgrad.T, gdown[None])


def solution(mesh):
    in_specs = (
        P(("dp", "expert"), None),
        P(("dp", "expert"), None),
        P(("dp", "expert"), None),
        P(("dp", "expert"), None),
        P("expert", "dp", None),
        P("expert", "dp", None),
        P("expert", None, "dp"),
    )
    out_specs = (
        P(("dp", "expert"), None),
        P(("dp", "expert"), None),
        P(("dp", "expert"), None),
        P("expert", None, "dp"),
    )
    return jax.shard_map(shards, mesh=mesh, in_specs=in_specs, out_specs=out_specs, check_vma=False)
```

```python
import functools
import jax
import jax.numpy as jnp
from jax import lax
from jax.experimental import pallas as pl
from jax.experimental.pallas import tpu as pltpu
from jax.sharding import PartitionSpec as P

CAP = 10
BF = jnp.bfloat16
F32 = jnp.float32
PLANE = [(1, 0), (0, 1), (3, 0), (0, 3), (2, 0), (0, 2), (1, 1), (3, 3),
         (1, 3), (3, 1), (2, 1), (1, 2), (2, 3), (3, 2), (2, 2)]


def dot_nn(a, b):
    return lax.dot_general(a, b, (((1,), (0,)), ((), ())), preferred_element_type=F32)


def dot_nt(a, b):
    return lax.dot_general(a, b, (((1,), (1,)), ((), ())), preferred_element_type=F32)


def iota(shape, dim):
    return lax.broadcasted_iota(jnp.int32, shape, dim)


def kernel(routes, rw, x, cot, wg, wu, wd, mixed, gtok, rgrad, gdown,
           W, WZ, sx, sc, rx, rc, RX, RC, H, GG, GU, OO, GP, po, pg, ro, rg, UO, UG, GT, GR, RS, S,
           wss, wrs, zss, zrs, tss, trs, bss, brs, gss, grs, rss, rrs):
    g = lax.axis_index("dp")
    s = lax.axis_index("expert")
    z, c = s // 2, lax.rem(s, 2)
    px, py = lax.rem(g, 4), g // 4
    me_e = jnp.where(c == 0, 2 * z, 2 * g + 1)

    def on_core(n):
        return pl.when(c == n)

    def plane(d):
        return lax.rem(py + d[1], 4) * 4 + lax.rem(px + d[0], 4)

    def dz(pos):
        return jnp.where(lax.rem(pos, 2) == 1, (pos + 1) // 2, lax.rem(16 - pos // 2, 16))

    def up_z(t):
        return lax.rem(z + t + 16, 16)

    bar = pltpu.get_barrier_semaphore()

    @pl.loop(1, 32)
    def _(d):
        pl.semaphore_signal(bar, inc=1, device_id=(g, lax.rem(s + d, 32)))

    @pl.loop(1, 16)
    def _(d):
        pl.semaphore_signal(bar, inc=1, device_id=(lax.rem(g + d, 16), 2 * z))
        pl.semaphore_signal(bar, inc=1, device_id=(lax.rem(g + d, 16), 2 * z + 1))

    eye = (iota((128, 128), 0) == iota((128, 128), 1))
    down_rows = dot_nt(eye.astype(BF), wd[...]).astype(BF)

    @on_core(0)
    def _():
        W[g, 0:128] = wg[...]
        W[g, 128:256] = wu[...]
        W[g, 256:384] = down_rows

    @on_core(1)
    def _():
        WZ[z, 0:128] = wg[...]
        WZ[z, 128:256] = wu[...]
        WZ[z, 256:384] = down_rows

    pl.semaphore_wait(bar, 31 + 30)

    def w_copy(core, i, r, n):
        p = plane(PLANE[i])
        src = W.at[g, pl.ds(r, n)] if core == 0 else WZ.at[p, pl.ds(r, n)]
        return pltpu.make_async_remote_copy(
            src, W.at[g, pl.ds(r, n)], wss.at[i], wrs.at[i], device_id=(p, s))

    def ring(way, t, h):
        to = up_z(1 - 2 * way)
        sl = lax.rem(z + 16 + (t if way else -t), 16)
        r = pl.ds(h * 192, 192)
        return pltpu.make_async_remote_copy(
            WZ.at[sl, r], WZ.at[sl, r], zss.at[way, t, h], zrs.at[way, t, h],
            device_id=(g, 2 * to + 1))

    def relay(t, last):
        for h in range(2):
            for way in range(2):
                ring(way, t - 1, h).wait_recv()
                if not last or h == way:
                    ring(way, t, h).start()

    @on_core(0)
    def _():
        @pl.loop(0, 12)
        def _(p):
            for i in range(15):
                w_copy(0, i, p * 32, 32).start()

    @on_core(1)
    def _():
        for h in range(2):
            for way in range(2):
                ring(way, 0, h).start()

    lanes = iota((128, 128), 1)

    def column(row):
        return jnp.sum(jnp.where(eye, row, 0.0), axis=1, keepdims=True)

    def row(col):
        return jnp.sum(jnp.where(eye, col, 0.0), axis=0, keepdims=True)

    w0, w1 = column(rw[0:1, :]), column(rw[1:2, :])
    e0, e1 = column(routes[0:1, :].astype(F32)), column(routes[1:2, :].astype(F32))
    r0, r1 = e0.astype(jnp.int32), e1.astype(jnp.int32)
    h0, h1 = (lanes == r0), (lanes == r1)
    named = (h0.astype(F32) + h1.astype(F32)).astype(BF)
    before = (iota((128, 128), 0) > lanes).astype(BF)
    count = dot_nn(before, named)
    t0 = e0 * CAP + jnp.sum(jnp.where(h0, count, 0.0), axis=1, keepdims=True)
    t1 = e1 * CAP + jnp.sum(jnp.where(h1, count, 0.0), axis=1, keepdims=True)
    u0, u1 = row(t0), row(t1)
    slots = iota((384, 128), 0).astype(F32)
    P0, P1 = (slots == u0).astype(BF), (slots == u1).astype(BF)

    S[...] = (iota((256, 256), 1) == lax.rem(iota((256, 256), 0), 16) * 16
              + iota((256, 256), 0) // 16).astype(BF)

    def pack(src, dst, lo, n):
        @pl.loop(0, n)
        def _(q):
            r = pl.multiple_of(lo + q * 32, 32)
            a = src[pl.ds(r, 32), :]
            cols = [jnp.concatenate([a[h * 16:h * 16 + 16, k * 128:k * 128 + 128] for k in range(16)], axis=0)
                    for h in range(2)]
            o = dot_nn(S[...], jnp.concatenate(cols, axis=1)).astype(BF)
            dst[pl.ds(r, 16)] = o[:, :128].reshape(16, 16, 128)
            dst[pl.ds(r + 16, 16)] = o[:, 128:].reshape(16, 16, 128)

    def unpack(src, dst, lo, n):
        @pl.loop(0, n)
        def _(q):
            r = pl.multiple_of(lo + q * 32, 32)
            a = src[pl.ds(r, 32)].reshape(512, 128)
            o = dot_nn(S[...], jnp.concatenate([a[:256], a[256:]], axis=1)).astype(BF)
            for h in range(2):
                dst[pl.ds(r + h * 16, 16), :] = jnp.concatenate(
                    [o[k * 16:k * 16 + 16, h * 128:h * 128 + 128] for k in range(16)], axis=1)

    def chip(pos, sign):
        dx, dy = lax.rem(pos, 4), pos // 4
        return lax.rem(py + sign * dy + 4, 4) * 4 + lax.rem(px + sign * dx + 4, 4)

    def tok(kind, pos, hc):
        src, dst = ((sx, rx), (sc, rc))[kind]
        if hc == 0:
            e = lax.rem(z + dz(pos), 16) * 2
            dev = (g, e)
        else:
            j = chip(pos, 1)
            e = 2 * j + 1
            dev = (j, 2 * z + 1)
        return pltpu.make_async_remote_copy(
            src.at[pl.ds(e * CAP, CAP)], dst.at[pl.ds((2 * pos + c) * CAP, CAP)],
            tss.at[kind, 2 * pos + hc], trs.at[kind, 2 * pos + c], device_id=dev)

    def tok_recv(kind, q):
        src, dst = ((sx, rx), (sc, rc))[kind]
        return pltpu.make_async_remote_copy(
            src.at[pl.ds(0, CAP)], dst.at[pl.ds(q * CAP, CAP)],
            tss.at[kind, q], trs.at[kind, q], device_id=(g, s + 1 - 2 * c))

    def send_tokens(kind, hc, first=0):
        if first == 0:
            @on_core(1 - hc)
            def _():
                tok(kind, 0, hc).start()

        @pl.loop(max(first, 1), 16)
        def _(pos):
            tok(kind, pos, hc).start()

    def keep(kind):
        src, dst = ((sx, rx), (sc, rc))[kind]
        dst[pl.ds(c * CAP, CAP)] = src[pl.ds(me_e * CAP, CAP)]

    pa = (P0.astype(F32) + P1.astype(F32)).astype(BF)

    @pl.loop(0, 8)
    def _(m):
        k = pl.ds(pl.multiple_of(m * 256, 256), 256)
        UO[:, k] = dot_nn(pa, x[:, k]).astype(BF)
    pack(UO, sx, 0, 10)
    keep(0)
    send_tokens(0, 1)

    @on_core(0)
    def _():
        send_tokens(0, 0)

    @on_core(1)
    def _():
        relay(1, False)

    @pl.loop(0, 8)
    def _(m):
        k = pl.ds(pl.multiple_of(m * 256, 256), 256)
        cf = cot[:, k].astype(F32)
        v0 = (cf * w0).astype(BF)
        v1 = (cf * w1).astype(BF)
        UG[:, k] = (dot_nn(P0, v0) + dot_nn(P1, v1)).astype(BF)
    pack(UG, sc, 0, 10)
    keep(1)
    send_tokens(1, 1)

    @on_core(0)
    def _():
        send_tokens(1, 0)

    @on_core(1)
    def _():
        @pl.loop(2, 7)
        def _(t):
            relay(t, False)
        relay(7, True)
        for way in range(2):
            ring(way, 7, way).wait_recv()
        W[g] = WZ[g]
        for kind in range(2):
            tok(kind, 0, 0).start()

        @pl.loop(0, 12)
        def _(p):
            for i in range(15):
                w_copy(1, i, p * 32, 32).start()
            for kind in range(2):
                tok(kind, p + 1, 0).start()
        for kind in range(2):
            send_tokens(kind, 0, 13)

    for i in range(15):
        w_copy(0, i, 0, 384).wait_recv()

    def back(kind, pos, cc):
        src, dst = ((po, ro), (pg, rg))[kind]
        dev = (jnp.where(c == 0, g, chip(pos, -1)),
               jnp.where(c == 0, lax.rem(z + 16 - dz(pos), 16), z) * 2 + cc)
        return pltpu.make_async_remote_copy(
            src.at[pl.ds((2 * pos + cc) * CAP, CAP)], dst.at[pl.ds(me_e * CAP, CAP)],
            bss.at[kind, 2 * pos + cc], brs.at[kind, me_e], device_id=dev)

    def back_recv(kind, e):
        src, dst = ((po, ro), (pg, rg))[kind]
        return pltpu.make_async_remote_copy(
            src.at[pl.ds(0, CAP)], dst.at[pl.ds(e * CAP, CAP)],
            bss.at[kind, e], brs.at[kind, e], device_id=(g, s + 1 - 2 * c))

    def phase_a(half):
        for kind in range(2):
            if half == 0:
                tok_recv(kind, 1 - c).wait_recv()

            @pl.loop(half * 16 + (2 if half == 0 else 0), half * 16 + 16)
            def _(q):
                tok_recv(kind, q).wait_recv()
        lo = half * 160
        unpack(rx, RX, lo, 5)
        unpack(rc, RC, lo, 5)
        rows = pl.ds(lo, 160)

        @pl.loop(0, 3)
        def _(n):
            k = pl.ds(pl.multiple_of(n * 256, 256), 256)
            xs, cs = RX[rows, :], RC[rows, :]
            gate = dot_nn(xs, W[:, 0:128, k].reshape(2048, 256))
            up = dot_nn(xs, W[:, 128:256, k].reshape(2048, 256))
            gh = dot_nn(cs, W[:, 256:384, k].reshape(2048, 256))
            sig = jax.nn.sigmoid(gate)
            act = gate * sig
            H[rows, k] = (act * up).astype(BF)
            GG[rows, k] = (gh * up * sig * (1.0 + gate * (1.0 - sig))).astype(BF)
            GU[rows, k] = (gh * act).astype(BF)

    def phase_b(half):
        lo = half * 160
        rows = pl.ds(lo, 160)

        @pl.loop(0, 8)
        def _(m):
            k = pl.ds(pl.multiple_of(m * 256, 256), 256)
            j = pl.ds(2 * m, 2)
            OO[rows, k] = dot_nt(H[rows, :], W[j, 256:384, :].reshape(256, 768)).astype(BF)
            GP[rows, k] = (dot_nt(GG[rows, :], W[j, 0:128, :].reshape(256, 768))
                           + dot_nt(GU[rows, :], W[j, 128:256, :].reshape(256, 768))).astype(BF)
        for kind in range(2):
            src, dst, flat = ((po, ro, OO), (pg, rg, GP))[kind]
            pack(flat, src, lo, 5)
            if half == 0:
                back(kind, 0, 1 - c).start()
                dst[pl.ds(me_e * CAP, CAP)] = src[pl.ds(c * CAP, CAP)]

            @pl.loop(half * 8 + (1 if half == 0 else 0), half * 8 + 8)
            def _(pos):
                back(kind, pos, 0).start()
                back(kind, pos, 1).start()

    def g_copy(i, r, n):
        p = plane(PLANE[i])
        return pltpu.make_async_remote_copy(
            GT.at[p, pl.ds(r, n)], GR.at[g, pl.ds(r, n)], gss.at[i], grs.at[g], device_id=(p, s))

    def g_recv(j):
        return pltpu.make_async_remote_copy(
            GT.at[j], GR.at[j], gss.at[0], grs.at[j], device_id=(g, s + 1 - 2 * c))

    def gradients():
        HT = jnp.transpose(H[...])

        @pl.loop(0, 8)
        def _(m):
            k = pl.ds(pl.multiple_of(m * 256, 256), 256)
            t = dot_nn(HT, RC[:, k]).astype(BF)
            GT[2 * m] = t[:, :128]
            GT[2 * m + 1] = t[:, 128:]

        @pl.loop(0, 4)
        def _(p):
            for i in range(15):
                g_copy(i, p * 192, 192).start()
        GR[g] = GT[g]

    def hop(way, t, h, first=False):
        to = up_z(1 - 2 * way)
        j = lax.rem(z + 16 + (t - 7 if way else 8 - t), 16)
        r = pl.ds(h * 384, 384)
        src = GR.at[j, r] if first else RS.at[way, t - 1, r]
        return j, pltpu.make_async_remote_copy(
            src, RS.at[way, t, r], rss.at[way, t, h], rrs.at[way, t, h], device_id=(g, 2 * to + 1))

    def g_wait(j):
        @pl.when(j != g)
        def _():
            g_recv(j).wait_recv()

    def reduce_z():
        for way in range(2):
            for h in range(2):
                j, cp = hop(way, 0, h, True)
                if h == 0:
                    g_wait(j)
                cp.start()

        def step(t, ways):
            for h in range(2):
                for way in ways:
                    j, cp = hop(way, t, h)
                    if h == 0:
                        g_wait(j)
                    hop(way, t - 1, h, True)[1].wait_recv()

                    @pl.loop(0, 6)
                    def _(b):
                        r = pl.ds(pl.multiple_of(h * 384 + b * 64, 64), 64)
                        RS[way, t - 1, r, :] = (RS[way, t - 1, r, :].astype(F32)
                                                + GR[j, r, :].astype(F32)).astype(BF)
                    cp.start()

        @pl.loop(1, 7)
        def _(t):
            step(t, (0, 1))
        step(7, (0,))
        g_wait(z)

    slots = iota((128, 384), 1).astype(F32)
    Q0, Q1 = (slots == t0).astype(BF), (slots == t1).astype(BF)
    qa = (Q0.astype(F32) + Q1.astype(F32)).astype(BF)

    def combine(kind):
        @pl.loop(0, 32)
        def _(e):
            @pl.when(e != me_e)
            def _():
                back_recv(kind, e).wait_recv()
        if kind == 0:
            UO[320:384, :] = jnp.zeros((64, 2048), BF)
            unpack(ro, UO, 0, 10)

            def body(m, carry):
                a0, a1 = carry
                k = pl.ds(pl.multiple_of(m * 256, 256), 256)
                o0, o1 = dot_nn(Q0, UO[:, k]), dot_nn(Q1, UO[:, k])
                mixed[:, k] = (w0 * o0 + w1 * o1).astype(BF)
                cf = cot[:, k].astype(F32)
                return (a0 + jnp.sum(cf * o0, axis=1, keepdims=True),
                        a1 + jnp.sum(cf * o1, axis=1, keepdims=True))
            a0, a1 = lax.fori_loop(0, 8, body, (jnp.zeros((128, 1), F32), jnp.zeros((128, 1), F32)))
            rgrad[0:1, :] = row(a0)
            rgrad[1:2, :] = row(a1)
        else:
            UG[320:384, :] = jnp.zeros((64, 2048), BF)
            unpack(rg, UG, 0, 10)

            @pl.loop(0, 8)
            def _(m):
                k = pl.ds(pl.multiple_of(m * 256, 256), 256)
                gtok[:, k] = dot_nn(qa, UG[:, k]).astype(BF)

    @on_core(0)
    def _():
        for half in range(2):
            phase_a(half)
            phase_b(half)
        gradients()

    @on_core(1)
    def _():
        phase_a(0)
        phase_a(1)
        gradients()
        phase_b(0)
        phase_b(1)
        reduce_z()

    combine(0)
    combine(1)

    @on_core(0)
    def _():
        @pl.loop(0, 16)
        def _(j):
            g_wait(j)

        @pl.loop(0, 12)
        def _(b):
            r = pl.ds(pl.multiple_of(b * 64, 64), 64)
            acc = GR[0, r, :].astype(F32)
            for i in range(1, 16):
                acc = acc + GR[i, r, :].astype(F32)
            gdown[r, :] = acc

    @on_core(1)
    def _():
        for h in range(2):
            hop(0, 7, h, True)[1].wait_recv()
            hop(1, 6, h, True)[1].wait_recv()

        @pl.loop(0, 12)
        def _(b):
            r = pl.ds(pl.multiple_of(b * 64, 64), 64)
            gdown[r, :] = (GR[z, r, :].astype(F32) + RS[0, 7, r, :].astype(F32)) + RS[1, 6, r, :].astype(F32)

    for i in range(15):
        w_copy(0, i, 0, 384).wait_send()
        g_copy(i, 0, 768).wait_send()
    for kind in range(2):
        @on_core(0)
        def _():
            tok(kind, 0, 1).wait_send()
            back(kind, 0, 1).wait_send()

        @on_core(1)
        def _():
            tok(kind, 0, 0).wait_send()
            back(kind, 0, 0).wait_send()

        @pl.loop(1, 16)
        def _(pos):
            for h in range(2):
                tok(kind, pos, h).wait_send()
                back(kind, pos, h).wait_send()

    @on_core(1)
    def _():
        for way in range(2):
            @pl.loop(0, 7)
            def _(t):
                for h in range(2):
                    ring(way, t, h).wait_send()
            ring(way, 7, way).wait_send()
            for h in range(2):
                hop(way, 0, h, True)[1].wait_send()

            @pl.loop(1, 8 - way)
            def _(t):
                for h in range(2):
                    hop(way, t, h, True)[1].wait_send()


def shards(tokens, cotangent, routes, route_weight, w_gate, w_up, w_down):
    rows, width = tokens.shape
    ff = w_gate.shape[2]
    part = w_gate.shape[1]
    tile = lambda: pltpu.VMEM((320, 16, 128), BF)
    flat = lambda n, w: pltpu.VMEM((n, w), BF)
    dma = pltpu.SemaphoreType.DMA
    out = pl.pallas_call(
        kernel,
        out_shape=(
            jax.ShapeDtypeStruct((rows, width), BF),
            jax.ShapeDtypeStruct((rows, width), BF),
            jax.ShapeDtypeStruct((2, rows), F32),
            jax.ShapeDtypeStruct((ff, part), F32),
        ),
        in_specs=[pl.BlockSpec(memory_space=pltpu.VMEM)] * 7,
        out_specs=[pl.BlockSpec(memory_space=pltpu.VMEM)] * 4,
        scratch_shapes=[
            pltpu.VMEM((16, 384, 768), BF), pltpu.VMEM((16, 384, 768), BF),
            tile(), tile(), tile(), tile(),
            flat(320, 2048), flat(320, 2048),
            flat(320, 768), flat(320, 768), flat(320, 768),
            flat(320, 2048), flat(320, 2048),
            tile(), tile(), tile(), tile(),
            flat(384, 2048), flat(384, 2048),
            pltpu.VMEM((16, 768, 128), BF), pltpu.VMEM((16, 768, 128), BF),
            pltpu.VMEM((2, 8, 768, 128), BF),
            flat(256, 256),
            dma((15,)), dma((15,)), dma((2, 8, 2)), dma((2, 8, 2)),
            dma((2, 32)), dma((2, 32)), dma((2, 32)), dma((2, 32)),
            dma((15,)), dma((16,)), dma((2, 8, 2)), dma((2, 8, 2)),
        ],
        compiler_params=pltpu.CompilerParams(
            collective_id=0, has_side_effects=True, vmem_limit_bytes=60 * 2**20),
    )(routes.T, route_weight.T, tokens, cotangent, w_gate[0], w_up[0], w_down[0])
    mixed, gtok, rgrad, gdown = out
    return (mixed, gtok, rgrad.T, gdown[None])


def solution(mesh):
    in_specs = (
        P(("dp", "expert"), None),
        P(("dp", "expert"), None),
        P(("dp", "expert"), None),
        P(("dp", "expert"), None),
        P("expert", "dp", None),
        P("expert", "dp", None),
        P("expert", None, "dp"),
    )
    out_specs = (
        P(("dp", "expert"), None),
        P(("dp", "expert"), None),
        P(("dp", "expert"), None),
        P("expert", None, "dp"),
    )
    return jax.shard_map(shards, mesh=mesh, in_specs=in_specs, out_specs=out_specs, check_vma=False)
```

```python
import functools
import jax
import jax.numpy as jnp
from jax import lax
from jax.experimental import pallas as pl
from jax.experimental.pallas import tpu as pltpu
from jax.sharding import PartitionSpec as P

CAP = 10
BF = jnp.bfloat16
F32 = jnp.float32
PLANE = [(1, 0), (0, 1), (3, 0), (0, 3), (2, 0), (0, 2), (1, 1), (3, 3),
         (1, 3), (3, 1), (2, 1), (1, 2), (2, 3), (3, 2), (2, 2)]


def dot_nn(a, b):
    return lax.dot_general(a, b, (((1,), (0,)), ((), ())), preferred_element_type=F32)


def dot_nt(a, b):
    return lax.dot_general(a, b, (((1,), (1,)), ((), ())), preferred_element_type=F32)


def iota(shape, dim):
    return lax.broadcasted_iota(jnp.int32, shape, dim)


def kernel(routes, rw, x, cot, wg, wu, wd, mixed, gtok, rgrad, gdown,
           W, WZ, sx, sc, rx, rc, RX, RC, H, GG, GU, OO, GP, po, pg, ro, rg, UO, UG, GT, GR, RS, S,
           wss, wrs, zss, zrs, tss, trs, bss, brs, gss, grs, rss, rrs):
    g = lax.axis_index("dp")
    s = lax.axis_index("expert")
    z, c = s // 2, lax.rem(s, 2)
    px, py = lax.rem(g, 4), g // 4
    me_e = jnp.where(c == 0, 2 * z, 2 * g + 1)

    def on_core(n):
        return pl.when(c == n)

    def plane(d):
        return lax.rem(py + d[1], 4) * 4 + lax.rem(px + d[0], 4)

    def dz(pos):
        return jnp.where(lax.rem(pos, 2) == 1, (pos + 1) // 2, lax.rem(16 - pos // 2, 16))

    def up_z(t):
        return lax.rem(z + t + 16, 16)

    bar = pltpu.get_barrier_semaphore()

    @pl.loop(1, 32)
    def _(d):
        pl.semaphore_signal(bar, inc=1, device_id=(g, lax.rem(s + d, 32)))

    @pl.loop(1, 16)
    def _(d):
        pl.semaphore_signal(bar, inc=1, device_id=(lax.rem(g + d, 16), 2 * z))
        pl.semaphore_signal(bar, inc=1, device_id=(lax.rem(g + d, 16), 2 * z + 1))

    eye = (iota((128, 128), 0) == iota((128, 128), 1))
    down_rows = dot_nt(eye.astype(BF), wd[...]).astype(BF)

    @on_core(0)
    def _():
        W[g, 0:128] = wg[...]
        W[g, 128:256] = wu[...]
        W[g, 256:384] = down_rows

    @on_core(1)
    def _():
        WZ[z, 0:128] = wg[...]
        WZ[z, 128:256] = wu[...]
        WZ[z, 256:384] = down_rows

    pl.semaphore_wait(bar, 31 + 30)

    def w_copy(core, i, r, n):
        p = plane(PLANE[i])
        src = W.at[g, pl.ds(r, n)] if core == 0 else WZ.at[p, pl.ds(r, n)]
        return pltpu.make_async_remote_copy(
            src, W.at[g, pl.ds(r, n)], wss.at[i], wrs.at[i], device_id=(p, s))

    def ring(way, t, h):
        to = up_z(1 - 2 * way)
        sl = lax.rem(z + 16 + (t if way else -t), 16)
        r = pl.ds(h * 192, 192)
        return pltpu.make_async_remote_copy(
            WZ.at[sl, r], WZ.at[sl, r], zss.at[way, t, h], zrs.at[way, t, h],
            device_id=(g, 2 * to + 1))

    def relay(t, last):
        for h in range(2):
            for way in range(2):
                ring(way, t - 1, h).wait_recv()
                if not last or h == way:
                    ring(way, t, h).start()

    @on_core(0)
    def _():
        @pl.loop(0, 12)
        def _(p):
            for i in range(15):
                w_copy(0, i, p * 32, 32).start()

    @on_core(1)
    def _():
        for h in range(2):
            for way in range(2):
                ring(way, 0, h).start()

    lanes = iota((128, 128), 1)

    def column(row):
        return jnp.sum(jnp.where(eye, row, 0.0), axis=1, keepdims=True)

    def row(col):
        return jnp.sum(jnp.where(eye, col, 0.0), axis=0, keepdims=True)

    w0, w1 = column(rw[0:1, :]), column(rw[1:2, :])
    e0, e1 = column(routes[0:1, :].astype(F32)), column(routes[1:2, :].astype(F32))
    r0, r1 = e0.astype(jnp.int32), e1.astype(jnp.int32)
    h0, h1 = (lanes == r0), (lanes == r1)
    named = (h0.astype(F32) + h1.astype(F32)).astype(BF)
    before = (iota((128, 128), 0) > lanes).astype(BF)
    count = dot_nn(before, named)
    t0 = e0 * CAP + jnp.sum(jnp.where(h0, count, 0.0), axis=1, keepdims=True)
    t1 = e1 * CAP + jnp.sum(jnp.where(h1, count, 0.0), axis=1, keepdims=True)
    u0, u1 = row(t0), row(t1)
    slots = iota((384, 128), 0).astype(F32)
    P0, P1 = (slots == u0).astype(BF), (slots == u1).astype(BF)

    S[...] = (iota((256, 256), 1) == lax.rem(iota((256, 256), 0), 16) * 16
              + iota((256, 256), 0) // 16).astype(BF)

    def pack(src, dst, lo, n):
        @pl.loop(0, n)
        def _(q):
            r = pl.multiple_of(lo + q * 32, 32)
            a = src[pl.ds(r, 32), :]
            cols = [jnp.concatenate([a[h * 16:h * 16 + 16, k * 128:k * 128 + 128] for k in range(16)], axis=0)
                    for h in range(2)]
            o = dot_nn(S[...], jnp.concatenate(cols, axis=1)).astype(BF)
            dst[pl.ds(r, 16)] = o[:, :128].reshape(16, 16, 128)
            dst[pl.ds(r + 16, 16)] = o[:, 128:].reshape(16, 16, 128)

    def unpack(src, dst, lo, n):
        @pl.loop(0, n)
        def _(q):
            r = pl.multiple_of(lo + q * 32, 32)
            a = src[pl.ds(r, 32)].reshape(512, 128)
            o = dot_nn(S[...], jnp.concatenate([a[:256], a[256:]], axis=1)).astype(BF)
            for h in range(2):
                dst[pl.ds(r + h * 16, 16), :] = jnp.concatenate(
                    [o[k * 16:k * 16 + 16, h * 128:h * 128 + 128] for k in range(16)], axis=1)

    def chip(pos, sign):
        dx, dy = lax.rem(pos, 4), pos // 4
        return lax.rem(py + sign * dy + 4, 4) * 4 + lax.rem(px + sign * dx + 4, 4)

    def tok(kind, pos, hc):
        src, dst = ((sx, rx), (sc, rc))[kind]
        if hc == 0:
            e = lax.rem(z + dz(pos), 16) * 2
            dev = (g, e)
        else:
            j = chip(pos, 1)
            e = 2 * j + 1
            dev = (j, 2 * z + 1)
        return pltpu.make_async_remote_copy(
            src.at[pl.ds(e * CAP, CAP)], dst.at[pl.ds((2 * pos + c) * CAP, CAP)],
            tss.at[kind, 2 * pos + hc], trs.at[kind, 2 * pos + c], device_id=dev)

    def tok_recv(kind, q):
        src, dst = ((sx, rx), (sc, rc))[kind]
        return pltpu.make_async_remote_copy(
            src.at[pl.ds(0, CAP)], dst.at[pl.ds(q * CAP, CAP)],
            tss.at[kind, q], trs.at[kind, q], device_id=(g, s + 1 - 2 * c))

    def send_tokens(kind, hc, first=0):
        if first == 0:
            @on_core(1 - hc)
            def _():
                tok(kind, 0, hc).start()

        @pl.loop(max(first, 1), 16)
        def _(pos):
            tok(kind, pos, hc).start()

    def keep(kind):
        src, dst = ((sx, rx), (sc, rc))[kind]
        dst[pl.ds(c * CAP, CAP)] = src[pl.ds(me_e * CAP, CAP)]

    pa = (P0.astype(F32) + P1.astype(F32)).astype(BF)

    @pl.loop(0, 8)
    def _(m):
        k = pl.ds(pl.multiple_of(m * 256, 256), 256)
        UO[:, k] = dot_nn(pa, x[:, k]).astype(BF)
    pack(UO, sx, 0, 10)
    keep(0)
    send_tokens(0, 1)

    @on_core(0)
    def _():
        send_tokens(0, 0)

    @on_core(1)
    def _():
        relay(1, False)

    @pl.loop(0, 8)
    def _(m):
        k = pl.ds(pl.multiple_of(m * 256, 256), 256)
        cf = cot[:, k].astype(F32)
        v0 = (cf * w0).astype(BF)
        v1 = (cf * w1).astype(BF)
        UG[:, k] = (dot_nn(P0, v0) + dot_nn(P1, v1)).astype(BF)
    pack(UG, sc, 0, 10)
    keep(1)
    send_tokens(1, 1)

    @on_core(0)
    def _():
        send_tokens(1, 0)

    @on_core(1)
    def _():
        @pl.loop(2, 7)
        def _(t):
            relay(t, False)
        relay(7, True)
        for way in range(2):
            ring(way, 7, way).wait_recv()
        W[g] = WZ[g]
        for kind in range(2):
            tok(kind, 0, 0).start()

        @pl.loop(0, 12)
        def _(p):
            for i in range(15):
                w_copy(1, i, p * 32, 32).start()
            for kind in range(2):
                tok(kind, p + 1, 0).start()
        for kind in range(2):
            send_tokens(kind, 0, 13)

    for i in range(15):
        w_copy(0, i, 0, 384).wait_recv()

    def back(kind, pos, cc):
        src, dst = ((po, ro), (pg, rg))[kind]
        dev = (jnp.where(c == 0, g, chip(pos, -1)),
               jnp.where(c == 0, lax.rem(z + 16 - dz(pos), 16), z) * 2 + cc)
        return pltpu.make_async_remote_copy(
            src.at[pl.ds((2 * pos + cc) * CAP, CAP)], dst.at[pl.ds(me_e * CAP, CAP)],
            bss.at[kind, 2 * pos + cc], brs.at[kind, me_e], device_id=dev)

    def back_recv(kind, e):
        src, dst = ((po, ro), (pg, rg))[kind]
        return pltpu.make_async_remote_copy(
            src.at[pl.ds(0, CAP)], dst.at[pl.ds(e * CAP, CAP)],
            bss.at[kind, e], brs.at[kind, e], device_id=(g, s + 1 - 2 * c))

    def phase_a(half):
        for kind in range(2):
            if half == 0:
                tok_recv(kind, 1 - c).wait_recv()

            @pl.loop(half * 16 + (2 if half == 0 else 0), half * 16 + 16)
            def _(q):
                tok_recv(kind, q).wait_recv()
        lo = half * 160
        unpack(rx, RX, lo, 5)
        unpack(rc, RC, lo, 5)
        rows = pl.ds(lo, 160)

        @pl.loop(0, 3)
        def _(n):
            k = pl.ds(pl.multiple_of(n * 256, 256), 256)
            xs, cs = RX[rows, :], RC[rows, :]
            gate = dot_nn(xs, W[:, 0:128, k].reshape(2048, 256))
            up = dot_nn(xs, W[:, 128:256, k].reshape(2048, 256))
            gh = dot_nn(cs, W[:, 256:384, k].reshape(2048, 256))
            sig = jax.nn.sigmoid(gate)
            act = gate * sig
            H[rows, k] = (act * up).astype(BF)
            GG[rows, k] = (gh * up * sig * (1.0 + gate * (1.0 - sig))).astype(BF)
            GU[rows, k] = (gh * act).astype(BF)

    def phase_b(half):
        lo = half * 160
        rows = pl.ds(lo, 160)

        @pl.loop(0, 8)
        def _(m):
            k = pl.ds(pl.multiple_of(m * 256, 256), 256)
            j = pl.ds(2 * m, 2)
            OO[rows, k] = dot_nt(H[rows, :], W[j, 256:384, :].reshape(256, 768)).astype(BF)
            GP[rows, k] = (dot_nt(GG[rows, :], W[j, 0:128, :].reshape(256, 768))
                           + dot_nt(GU[rows, :], W[j, 128:256, :].reshape(256, 768))).astype(BF)
        for kind in range(2):
            src, dst, flat = ((po, ro, OO), (pg, rg, GP))[kind]
            pack(flat, src, lo, 5)
            if half == 0:
                back(kind, 0, 1 - c).start()
                dst[pl.ds(me_e * CAP, CAP)] = src[pl.ds(c * CAP, CAP)]

            @pl.loop(half * 8 + (1 if half == 0 else 0), half * 8 + 8)
            def _(pos):
                back(kind, pos, 0).start()
                back(kind, pos, 1).start()

    def g_copy(i, r, n):
        p = plane(PLANE[i])
        return pltpu.make_async_remote_copy(
            GT.at[p, pl.ds(r, n)], GR.at[g, pl.ds(r, n)], gss.at[i], grs.at[g], device_id=(p, s))

    def g_recv(j):
        return pltpu.make_async_remote_copy(
            GT.at[j], GR.at[j], gss.at[0], grs.at[j], device_id=(g, s + 1 - 2 * c))

    def gradients():
        HT = jnp.transpose(H[...])

        @pl.loop(0, 8)
        def _(m):
            k = pl.ds(pl.multiple_of(m * 256, 256), 256)
            t = dot_nn(HT, RC[:, k]).astype(BF)
            GT[2 * m] = t[:, :128]
            GT[2 * m + 1] = t[:, 128:]

        @pl.loop(0, 4)
        def _(p):
            for i in range(15):
                g_copy(i, p * 192, 192).start()
        GR[g] = GT[g]

    def hop(way, t, h, first=False):
        to = up_z(1 - 2 * way)
        j = lax.rem(z + 16 + (t - 7 if way else 8 - t), 16)
        r = pl.ds(h * 192, 192)
        src = GR.at[j, r] if first else RS.at[way, t - 1, r]
        return j, pltpu.make_async_remote_copy(
            src, RS.at[way, t, r], rss.at[way, t, h], rrs.at[way, t, h], device_id=(g, 2 * to + 1))

    def g_wait(j):
        @pl.when(j != g)
        def _():
            g_recv(j).wait_recv()

    def reduce_z():
        for way in range(2):
            for h in range(4):
                j, cp = hop(way, 0, h, True)
                if h == 0:
                    g_wait(j)
                cp.start()

        def step(t, ways):
            for h in range(4):
                for way in ways:
                    j, cp = hop(way, t, h)
                    if h == 0:
                        g_wait(j)
                    hop(way, t - 1, h, True)[1].wait_recv()

                    @pl.loop(0, 3)
                    def _(b):
                        r = pl.ds(pl.multiple_of(h * 192 + b * 64, 64), 64)
                        RS[way, t - 1, r, :] = (RS[way, t - 1, r, :].astype(F32)
                                                + GR[j, r, :].astype(F32)).astype(BF)
                    cp.start()

        @pl.loop(1, 7)
        def _(t):
            step(t, (0, 1))
        step(7, (0,))
        g_wait(z)

    slots = iota((128, 384), 1).astype(F32)
    Q0, Q1 = (slots == t0).astype(BF), (slots == t1).astype(BF)
    qa = (Q0.astype(F32) + Q1.astype(F32)).astype(BF)

    def combine(kind):
        @pl.loop(0, 32)
        def _(e):
            @pl.when(e != me_e)
            def _():
                back_recv(kind, e).wait_recv()
        if kind == 0:
            UO[320:384, :] = jnp.zeros((64, 2048), BF)
            unpack(ro, UO, 0, 10)

            def body(m, carry):
                a0, a1 = carry
                k = pl.ds(pl.multiple_of(m * 256, 256), 256)
                o0, o1 = dot_nn(Q0, UO[:, k]), dot_nn(Q1, UO[:, k])
                mixed[:, k] = (w0 * o0 + w1 * o1).astype(BF)
                cf = cot[:, k].astype(F32)
                return (a0 + jnp.sum(cf * o0, axis=1, keepdims=True),
                        a1 + jnp.sum(cf * o1, axis=1, keepdims=True))
            a0, a1 = lax.fori_loop(0, 8, body, (jnp.zeros((128, 1), F32), jnp.zeros((128, 1), F32)))
            rgrad[0:1, :] = row(a0)
            rgrad[1:2, :] = row(a1)
        else:
            UG[320:384, :] = jnp.zeros((64, 2048), BF)
            unpack(rg, UG, 0, 10)

            @pl.loop(0, 8)
            def _(m):
                k = pl.ds(pl.multiple_of(m * 256, 256), 256)
                gtok[:, k] = dot_nn(qa, UG[:, k]).astype(BF)

    @on_core(0)
    def _():
        for half in range(2):
            phase_a(half)
            phase_b(half)
        gradients()

    @on_core(1)
    def _():
        phase_a(0)
        phase_a(1)
        gradients()
        phase_b(0)
        phase_b(1)
        reduce_z()

    combine(0)
    combine(1)

    @on_core(0)
    def _():
        @pl.loop(0, 16)
        def _(j):
            g_wait(j)

        @pl.loop(0, 12)
        def _(b):
            r = pl.ds(pl.multiple_of(b * 64, 64), 64)
            acc = GR[0, r, :].astype(F32)
            for i in range(1, 16):
                acc = acc + GR[i, r, :].astype(F32)
            gdown[r, :] = acc

    @on_core(1)
    def _():
        for h in range(4):
            hop(0, 7, h, True)[1].wait_recv()
            hop(1, 6, h, True)[1].wait_recv()

        @pl.loop(0, 12)
        def _(b):
            r = pl.ds(pl.multiple_of(b * 64, 64), 64)
            gdown[r, :] = (GR[z, r, :].astype(F32) + RS[0, 7, r, :].astype(F32)) + RS[1, 6, r, :].astype(F32)

    for i in range(15):
        w_copy(0, i, 0, 384).wait_send()
        g_copy(i, 0, 768).wait_send()
    for kind in range(2):
        @on_core(0)
        def _():
            tok(kind, 0, 1).wait_send()
            back(kind, 0, 1).wait_send()

        @on_core(1)
        def _():
            tok(kind, 0, 0).wait_send()
            back(kind, 0, 0).wait_send()

        @pl.loop(1, 16)
        def _(pos):
            for h in range(2):
                tok(kind, pos, h).wait_send()
                back(kind, pos, h).wait_send()

    @on_core(1)
    def _():
        for way in range(2):
            @pl.loop(0, 7)
            def _(t):
                for h in range(2):
                    ring(way, t, h).wait_send()
            ring(way, 7, way).wait_send()
            for h in range(4):
                hop(way, 0, h, True)[1].wait_send()

            @pl.loop(1, 8 - way)
            def _(t):
                for h in range(4):
                    hop(way, t, h, True)[1].wait_send()


def shards(tokens, cotangent, routes, route_weight, w_gate, w_up, w_down):
    rows, width = tokens.shape
    ff = w_gate.shape[2]
    part = w_gate.shape[1]
    tile = lambda: pltpu.VMEM((320, 16, 128), BF)
    flat = lambda n, w: pltpu.VMEM((n, w), BF)
    dma = pltpu.SemaphoreType.DMA
    out = pl.pallas_call(
        kernel,
        out_shape=(
            jax.ShapeDtypeStruct((rows, width), BF),
            jax.ShapeDtypeStruct((rows, width), BF),
            jax.ShapeDtypeStruct((2, rows), F32),
            jax.ShapeDtypeStruct((ff, part), F32),
        ),
        in_specs=[pl.BlockSpec(memory_space=pltpu.VMEM)] * 7,
        out_specs=[pl.BlockSpec(memory_space=pltpu.VMEM)] * 4,
        scratch_shapes=[
            pltpu.VMEM((16, 384, 768), BF), pltpu.VMEM((16, 384, 768), BF),
            tile(), tile(), tile(), tile(),
            flat(320, 2048), flat(320, 2048),
            flat(320, 768), flat(320, 768), flat(320, 768),
            flat(320, 2048), flat(320, 2048),
            tile(), tile(), tile(), tile(),
            flat(384, 2048), flat(384, 2048),
            pltpu.VMEM((16, 768, 128), BF), pltpu.VMEM((16, 768, 128), BF),
            pltpu.VMEM((2, 8, 768, 128), BF),
            flat(256, 256),
            dma((15,)), dma((15,)), dma((2, 8, 2)), dma((2, 8, 2)),
            dma((2, 32)), dma((2, 32)), dma((2, 32)), dma((2, 32)),
            dma((15,)), dma((16,)), dma((2, 8, 4)), dma((2, 8, 4)),
        ],
        compiler_params=pltpu.CompilerParams(
            collective_id=0, has_side_effects=True, vmem_limit_bytes=60 * 2**20),
    )(routes.T, route_weight.T, tokens, cotangent, w_gate[0], w_up[0], w_down[0])
    mixed, gtok, rgrad, gdown = out
    return (mixed, gtok, rgrad.T, gdown[None])


def solution(mesh):
    in_specs = (
        P(("dp", "expert"), None),
        P(("dp", "expert"), None),
        P(("dp", "expert"), None),
        P(("dp", "expert"), None),
        P("expert", "dp", None),
        P("expert", "dp", None),
        P("expert", None, "dp"),
    )
    out_specs = (
        P(("dp", "expert"), None),
        P(("dp", "expert"), None),
        P(("dp", "expert"), None),
        P("expert", None, "dp"),
    )
    return jax.shard_map(shards, mesh=mesh, in_specs=in_specs, out_specs=out_specs, check_vma=False)
```
